32 devices in a mesh: layer: 8 (over z, core), dp: 4 (over y, x).
Axes of the slice: x: 2, y: 2, z: 4, core: 2. Of those that a mesh axis runs over, the one named last changes fastest.
Arguments:
- starts: float32 [8, 4, 32, 32, 128], P('layer', 'dp'), may hold values from -6 to 6
- weights: bfloat16 [32, 9, 128, 128], P('layer'), may hold values from -0.1875 to 0.1875
- biases: bfloat16 [32, 128], P('layer'), may hold values from -3 to 3
- adj_ends: float32 [8, 4, 32, 32, 128], P('layer', 'dp'), may hold values from -6 to 6
Outputs:
- block_ends: float32 [8, 4, 32, 32, 128], P('layer', 'dp')
- adjoint_starts: float32 [8, 4, 32, 32, 128], P('layer', 'dp')
- weight_grad: float32 [32, 9, 128, 128], P('layer')
- bias_grad: float32 [32, 128], P('layer')
The draws below stay inside these ranges and needn't reach their ends.
All inputs are finite; a program needn't handle non-finite values.
Results may differ from the reference program's by a relative error of at most 0.039.
Values may be sent and summed in bfloat16 or wider, within the bound.
A program may use at most 64 MiB of HBM per device.

```python
import math
import jax
import jax.numpy as jnp
from jax import lax

C = 128
MAP = 32
LAYERS = 32
IMAGES = 4
N_LAYER = 8


def level_of(stream_key, dims, cuts, smallest, largest):
    loudness = 1.0
    for axis_at, shards_of in cuts:
        steps = jax.random.uniform(jax.random.fold_in(jax.random.fold_in(stream_key, 6), axis_at), (shards_of,), jnp.float32, smallest / len(cuts), largest / len(cuts))
        loudness = loudness * jnp.repeat(jnp.exp(steps), dims[axis_at] // shards_of).reshape((-1,) + (1,) * (len(dims) - 1 - axis_at))
    return loudness


def noise(stream_key, shape, spread, reach, cuts=(), dtype=jnp.bfloat16):
    loudness = level_of(stream_key, shape, cuts, -0.22, 0.18) if cuts else 1.0
    array = jax.random.normal(stream_key, shape, jnp.float32) * spread * loudness
    return jnp.minimum(jnp.maximum(array, -reach), reach).astype(dtype)


def setup_inputs(seed: int = 0) -> dict:
    streams_of = jax.random.split(jax.random.key(seed), 5)
    starts = noise(streams_of[0], (N_LAYER, IMAGES, MAP, MAP, C), 1.0, 6.0, ((0, 8), (1, 4)), jnp.float32)
    weights = noise(streams_of[1], (LAYERS, 9, C, C), (9 * C) ** -0.5, 0.1875, ((0, 8),))
    biases = noise(streams_of[2], (LAYERS, C), 0.5, 3.0, ((0, 8),))
    adj_ends = noise(streams_of[3], (N_LAYER, IMAGES, MAP, MAP, C), 1.0, 6.0, ((0, 8), (1, 4)), jnp.float32)
    return {"starts": starts, "weights": weights, "biases": biases, "adj_ends": adj_ends}


step_size = 0.25

def convolve(rounded, kernel):
    count, map_side, _, channels = rounded.shape
    padded = jnp.pad(rounded, ((0, 0), (1, 1), (1, 1), (0, 0)))
    running = jnp.zeros((count * map_side * map_side, kernel.shape[2]), jnp.float32)
    for tap_index in range(9):
        row_off = tap_index // 3
        col_off = tap_index % 3
        view = padded[:, row_off:row_off + map_side, col_off:col_off + map_side, :].reshape(count * map_side * map_side, channels)
        running = running + jnp.dot(view, kernel[tap_index], preferred_element_type=jnp.float32)
    return running.reshape(count, map_side, map_side, kernel.shape[2])

def transposed(signal, kernel):
    count, map_side, _, channels = signal.shape
    padded = jnp.pad(signal, ((0, 0), (1, 1), (1, 1), (0, 0)))
    running = jnp.zeros((count * map_side * map_side, kernel.shape[1]), jnp.float32)
    for tap_index in range(9):
        row_off = 2 - tap_index // 3
        col_off = 2 - tap_index % 3
        view = padded[:, row_off:row_off + map_side, col_off:col_off + map_side, :].reshape(count * map_side * map_side, channels)
        running = running + lax.dot_general(view, kernel[tap_index], (((1,), (1,)), ((), ())), preferred_element_type=jnp.float32)
    return running.reshape(count, map_side, map_side, kernel.shape[1])

def correlate(rounded, signal):
    count, map_side, _, channels = rounded.shape
    padded = jnp.pad(rounded, ((0, 0), (1, 1), (1, 1), (0, 0)))
    flat_signal = signal.reshape(count * map_side * map_side, signal.shape[3])
    pieces = []
    for tap_index in range(9):
        row_off = tap_index // 3
        col_off = tap_index % 3
        view = padded[:, row_off:row_off + map_side, col_off:col_off + map_side, :].reshape(count * map_side * map_side, channels)
        pieces.append(lax.dot_general(view, flat_signal, (((0,), (0,)), ((), ())), preferred_element_type=jnp.float32))
    return jnp.stack(pieces)

def activation_of(current_state, kernel, bias_row):
    preact = convolve(current_state.astype(jnp.bfloat16), kernel) + bias_row.astype(jnp.float32)
    return jnp.tanh(preact)

def reference(starts, weights, biases, adj_ends):
    blocks = starts.shape[0]
    block_depth = weights.shape[0] // blocks
    coarse_step = block_depth * step_size
    map_side = starts.shape[2]
    grad_scale = 1.0 / (map_side * math.sqrt(starts.shape[1]))
    relaxed = []
    for block_pos in range(blocks):
        current_state = starts[block_pos]
        for inner_pos in range(block_depth):
            layer_pos = block_pos * block_depth + inner_pos
            current_state = current_state + step_size * activation_of(current_state, weights[layer_pos], biases[layer_pos])
        relaxed.append(current_state)

    def coarse_apply(current_state, block_pos):
        layer_pos = block_pos * block_depth
        return current_state + coarse_step * activation_of(current_state, weights[layer_pos], biases[layer_pos])
    coarse_list = [starts[0]]
    for block_pos in range(blocks - 1):
        coarse_list.append(relaxed[block_pos] - coarse_apply(starts[block_pos], block_pos) + coarse_apply(coarse_list[block_pos], block_pos))
    fine_states = []
    activations = []
    ends_list = []
    for block_pos in range(blocks):
        current_state = coarse_list[block_pos]
        for inner_pos in range(block_depth):
            layer_pos = block_pos * block_depth + inner_pos
            fine_states.append(current_state)
            activation = activation_of(current_state, weights[layer_pos], biases[layer_pos])
            activations.append(activation)
            current_state = current_state + step_size * activation
        ends_list.append(current_state)
    backed = []
    for block_pos in range(blocks):
        adjoint = adj_ends[block_pos]
        for inner_pos in reversed(range(block_depth)):
            layer_pos = block_pos * block_depth + inner_pos
            activation = activations[layer_pos]
            signal = ((1.0 - activation * activation) * adjoint).astype(jnp.bfloat16)
            adjoint = adjoint + step_size * transposed(signal, weights[layer_pos])
        backed.append(adjoint)
    exits = [None] * blocks
    exits[blocks - 1] = adj_ends[blocks - 1]
    for block_pos in range(blocks - 1, 0, -1):
        layer_pos = block_pos * block_depth
        activation = activations[layer_pos]
        difference = exits[block_pos] - adj_ends[block_pos]
        signal = ((1.0 - activation * activation) * difference).astype(jnp.bfloat16)
        exits[block_pos - 1] = backed[block_pos] + (difference + coarse_step * transposed(signal, weights[layer_pos]))
    starts_list = []
    kernel_grads = [None] * weights.shape[0]
    bias_grads = [None] * weights.shape[0]
    for block_pos in range(blocks):
        adjoint = exits[block_pos]
        for inner_pos in reversed(range(block_depth)):
            layer_pos = block_pos * block_depth + inner_pos
            activation = activations[layer_pos]
            signal = ((1.0 - activation * activation) * adjoint).astype(jnp.bfloat16)
            kernel_grads[layer_pos] = correlate(fine_states[layer_pos].astype(jnp.bfloat16), signal) * grad_scale
            bias_grads[layer_pos] = lax.optimization_barrier(jnp.sum(signal.astype(jnp.float32), axis=(0, 1, 2))) * grad_scale
            adjoint = adjoint + step_size * transposed(signal, weights[layer_pos])
        starts_list.append(adjoint)
    return (jnp.stack(ends_list), jnp.stack(starts_list), jnp.stack(kernel_grads), jnp.stack(bias_grads))
```

```python
import functools
import math

import jax
import jax.numpy as jnp
from jax import lax
from jax.experimental import pallas as pl
from jax.experimental.pallas import tpu as pltpu
from jax.sharding import PartitionSpec as P

step_size = 0.25
MESH = pl.DeviceIdType.MESH
f32 = jnp.float32
bf16 = jnp.bfloat16


def kernel(
    cfg,
    starts, weights, biases, adj_ends,
    ends, adj_starts, wgrad, bgrad,
    a3f, a3s, slope, offs, ent, ext, txf, txb, wt, a3t, brow,
    gsend, grx, gred, bias_all,
    fsend, frecv, bsend, brecv, rs_send, rs_recv, ag_send, ag_recv, bi_send, bi_recv,
):
    blocks, peers, depth, side, chans, groups, bands, chunk = cfg
    pix = side * side
    pad = side
    taps = 9 * chans
    per_group = depth // groups
    group_rows = per_group * taps
    share = group_rows // peers
    coarse_step = depth * step_size
    grad_scale = 1.0 / (side * math.sqrt(peers))
    band = pix // bands

    k = lax.axis_index("layer")
    me = lax.axis_index("dp")
    first = k == 0
    last = k == blocks - 1
    peer = [lax.rem(me + d, peers) for d in range(1, peers)]

    barrier = pltpu.get_barrier_semaphore()

    @pl.when(jnp.logical_not(first))
    def _():
        pl.semaphore_signal(barrier, inc=1, device_id={"layer": k - 1}, device_id_type=MESH)

    @pl.when(jnp.logical_not(last))
    def _():
        pl.semaphore_signal(barrier, inc=1, device_id={"layer": k + 1}, device_id_type=MESH)

    for p in peer:
        pl.semaphore_signal(barrier, inc=1, device_id={"dp": p}, device_id_type=MESH)
    greeted = (peers - 1) + jnp.where(first, 0, 1) + jnp.where(last, 0, 1)

    def put3(dst, row, val):
        rows = val.shape[0]
        col = lax.rem(lax.broadcasted_iota(jnp.int32, (rows, chans), 0), side)
        before = jnp.where(col == 0, 0.0, pltpu.roll(val, 1, 0))
        after = jnp.where(col == side - 1, 0.0, pltpu.roll(val, rows - 1, 0))
        at = pl.ds(pad + row, rows)
        dst[at, 0:chans] = before.astype(bf16)
        dst[at, chans : 2 * chans] = val.astype(bf16)
        dst[at, 2 * chans : 3 * chans] = after.astype(bf16)

    def conv(src, row, rows, mat):
        lhs = jnp.concatenate([src[pl.ds(row + e * side, rows), :] for e in range(3)], axis=1)
        return jnp.dot(lhs, mat, preferred_element_type=f32)

    bias32 = biases[...].astype(f32)
    for i in range(depth):
        brow[i] = bias32[i : i + 1]
    zeros = jnp.zeros((pad, 3 * chans), bf16)
    for i in range(depth + 1):
        a3f[i, 0:pad] = zeros
        a3f[i, pad + pix : 2 * pad + pix] = zeros
    for i in range(2):
        a3s[i, 0:pad] = zeros
        a3s[i, pad + pix : 2 * pad + pix] = zeros

    chunks = list(range(0, pix, chunk))

    for r in chunks:
        put3(a3f.at[0], r, starts[r : r + chunk])
    for r in chunks:
        act = jnp.tanh(conv(a3f.at[0], r, chunk, weights[0]) + brow[0])
        slope[0, r : r + chunk] = 1.0 - act * act
        u0 = starts[r : r + chunk]
        u1 = u0 + step_size * act
        offs[r : r + chunk] = u0 + coarse_step * act
        ends[r : r + chunk] = u1
        put3(a3f.at[1], r, u1)

    def forward_layer(i, _):
        for r in chunks:
            act = jnp.tanh(conv(a3f.at[i], r, chunk, weights[i]) + brow[i])
            slope[i, r : r + chunk] = 1.0 - act * act
            u = ends[r : r + chunk] + step_size * act
            ends[r : r + chunk] = u
            put3(a3f.at[i + 1], r, u)
        return 0

    lax.fori_loop(1, depth, forward_layer, 0)
    for r in chunks:
        offs[r : r + chunk] = ends[r : r + chunk] - offs[r : r + chunk]

    def turn_weights():
        def one(i, _):
            for t in range(9):
                wt[i, t * chans : (t + 1) * chans] = weights[i, (8 - t) * chans : (9 - t) * chans].T
            return 0

        lax.fori_loop(0, depth, one, 0)

    def turn_states():
        def one(i, _):
            for d in range(3):
                for r in range(0, pix, chans):
                    a3t[i, d * chans : (d + 1) * chans, r : r + chans] = a3f[
                        i, pad + r : pad + r + chans, d * chans : (d + 1) * chans
                    ].T
            return 0

        lax.fori_loop(0, depth, one, 0)

    early = k < blocks // 2
    late = jnp.logical_not(early)
    pl.when(late)(turn_weights)

    pl.semaphore_wait(barrier, greeted)

    def hop(src, dst, send, recv, b, to):
        at = pl.ds(b * band, band)
        return pltpu.make_async_remote_copy(
            src_ref=src.at[at], dst_ref=dst.at[at], send_sem=send.at[b], recv_sem=recv.at[b],
            device_id={"layer": to}, device_id_type=MESH,
        )

    up = lax.rem(k + 1, blocks)
    down = lax.rem(k + blocks - 1, blocks)
    fwd = [hop(txf, ent, fsend, frecv, b, up) for b in range(bands)]
    bwd = [hop(txb, ext, bsend, brecv, b, down) for b in range(bands)]

    @pl.when(first)
    def _():
        for b in range(bands):
            at = pl.ds(b * band, band)
            txf[at] = ends[at].astype(bf16)
            fwd[b].start()

    @pl.when(jnp.logical_not(first))
    def _():
        def work(b):
            at = pl.ds(b * band, band)
            act = jnp.tanh(conv(a3f.at[0], b * band, band, weights[0]) + brow[0])
            state = ent[at].astype(f32)

            @pl.when(jnp.logical_not(last))
            def _():
                txf[at] = (offs[at] + (state + coarse_step * act)).astype(bf16)
                fwd[b].start()

            slope[0, at] = 1.0 - act * act
            u = state + step_size * act
            ends[at] = u
            put3(a3f.at[1], b * band, u)

        for b in range(bands):
            fwd[b].wait_recv()
            put3(a3f.at[0], b * band, ent[pl.ds(b * band, band)].astype(f32))
            if b:
                work(b - 1)
        work(bands - 1)
        lax.fori_loop(1, depth, forward_layer, 0)

    pl.when(early)(turn_weights)

    top = depth - 1
    for r in chunks:
        l = adj_ends[r : r + chunk]
        adj_starts[r : r + chunk] = l
        put3(a3s.at[top % 2], r, slope[top, r : r + chunk] * l)

    def adjoint_layer(i):
        now = lax.rem(i, 2)
        below = jnp.maximum(i - 1, 0)
        for r in chunks:
            l = adj_starts[r : r + chunk] + step_size * conv(a3s.at[now], r, chunk, wt[i])
            adj_starts[r : r + chunk] = l
            put3(a3s.at[1 - now], r, slope[below, r : r + chunk] * l)

    def back_layer(j, _):
        adjoint_layer(top - j)
        return 0

    lax.fori_loop(0, depth, back_layer, 0)

    @pl.when(last)
    def _():
        for b in range(bands):
            at = pl.ds(b * band, band)
            txb[at] = adj_starts[at].astype(bf16)
            bwd[b].start()

    pl.when(early)(turn_states)

    @pl.when(jnp.logical_not(last))
    def _():
        @pl.when(jnp.logical_not(first))
        def _():
            def work(b):
                at = pl.ds(b * band, band)
                diff = ext[at].astype(f32) - adj_ends[at]
                out = adj_starts[at] + (diff + coarse_step * conv(a3s.at[0], b * band, band, wt[0]))
                txb[at] = out.astype(bf16)
                bwd[b].start()

            for b in range(bands):
                at = pl.ds(b * band, band)
                bwd[b].wait_recv()
                put3(a3s.at[0], b * band, slope[0, at] * (ext[at].astype(f32) - adj_ends[at]))
                if b:
                    work(b - 1)
            work(bands - 1)

        @pl.when(first)
        def _():
            for b in range(bands):
                bwd[b].wait_recv()

        for r in chunks:
            adj_starts[r : r + chunk] = ext[r : r + chunk].astype(f32)

    @pl.when(last)
    def _():
        for r in chunks:
            adj_starts[r : r + chunk] = adj_ends[r : r + chunk]

    for r in chunks:
        put3(a3s.at[top % 2], r, slope[top, r : r + chunk] * adj_starts[r : r + chunk])
    pl.when(late)(turn_states)

    mine = pl.ds(pl.multiple_of(me * share, share), share)

    def scatter(g, d):
        theirs = pl.ds(pl.multiple_of(peer[d] * share, share), share)
        return pltpu.make_async_remote_copy(
            src_ref=gsend.at[g, theirs], dst_ref=grx.at[g, d],
            send_sem=rs_send.at[g, d], recv_sem=rs_recv.at[g, d],
            device_id={"dp": peer[d]}, device_id_type=MESH,
        )

    def gather(g, d):
        return pltpu.make_async_remote_copy(
            src_ref=gred.at[g, mine], dst_ref=gred.at[g, mine],
            send_sem=ag_send.at[g, d], recv_sem=ag_recv.at[g, d],
            device_id={"dp": peer[d]}, device_id_type=MESH,
        )

    def bias_copy(d):
        return pltpu.make_async_remote_copy(
            src_ref=bias_all.at[me], dst_ref=bias_all.at[me],
            send_sem=bi_send.at[d], recv_sem=bi_recv.at[d],
            device_id={"dp": peer[d]}, device_id_type=MESH,
        )

    def reduce_group(g):
        for d in range(peers - 1):
            scatter(g, d).wait_recv()
        total = gsend[g, mine].astype(f32)
        for d in range(peers - 1):
            total = total + grx[g, d].astype(f32)
        gred[g, mine] = total.astype(bf16)
        for d in range(peers - 1):
            gather(g, d).start()

    def final_group(j, _):
        g = groups - 1 - j
        for q in reversed(range(per_group)):
            i = g * per_group + q
            now = lax.rem(i, 2)
            sig = a3s.at[now]
            rhs = jnp.concatenate(
                [sig[(2 - e) * side : (2 - e) * side + pix, chans : 2 * chans] for e in range(3)], axis=1
            )
            found = jnp.dot(a3t[i], rhs, preferred_element_type=f32) * grad_scale
            for e in range(3):
                for d in range(3):
                    to = q * taps + (3 * e + d) * chans
                    gsend[g, to : to + chans] = found[
                        d * chans : (d + 1) * chans, e * chans : (e + 1) * chans
                    ].astype(bf16)
            summed = jnp.sum(sig[pad : pad + pix, chans : 2 * chans].astype(f32), axis=0, keepdims=True)
            brow[i] = summed * grad_scale
            if q == 0:
                for d in range(peers - 1):
                    scatter(g, d).start()
            adjoint_layer(i)

        @pl.when(j > 0)
        def _():
            reduce_group(jnp.minimum(g + 1, groups - 1))

        return 0

    lax.fori_loop(0, groups, final_group, 0)
    for i in range(depth):
        bias_all[me, i : i + 1] = brow[i]
    for d in range(peers - 1):
        bias_copy(d).start()
    reduce_group(0)

    for d in range(peers - 1):
        bias_copy(d).wait_recv()
    total = bias_all[0, 0:depth]
    for p in range(1, peers):
        total = total + bias_all[p, 0:depth]
    bgrad[...] = total

    def finish(j, _):
        g = groups - 1 - j
        for d in range(peers - 1):
            gather(g, d).wait_recv()
        for q in range(per_group):
            wgrad[g * per_group + q] = gred[g, q * taps : (q + 1) * taps].astype(f32)
        return 0

    lax.fori_loop(0, groups, finish, 0)

    @pl.when(jnp.logical_not(last))
    def _():
        for b in range(bands):
            fwd[b].wait_send()

    @pl.when(jnp.logical_not(first))
    def _():
        for b in range(bands):
            bwd[b].wait_send()

    def drain(g, _):
        for d in range(peers - 1):
            scatter(g, d).wait_send()
            gather(g, d).wait_send()
        return 0

    lax.fori_loop(0, groups, drain, 0)
    for d in range(peers - 1):
        bias_copy(d).wait_send()


def local(blocks, peers, starts, weights, biases, adj_ends):
    _, _, side, _, chans = starts.shape
    depth = weights.shape[0]
    pix = side * side
    taps = 9 * chans
    bands = 4
    chunk = min(256, pix)
    groups = max(
        g for g in range(1, depth + 1)
        if depth % g == 0 and (depth // g * taps) % (16 * peers) == 0
    )
    group_rows = depth // groups * taps
    share = group_rows // peers
    cfg = (blocks, peers, depth, side, chans, groups, bands, chunk)
    padded = pix + 2 * side
    vmem = pl.BlockSpec(memory_space=pltpu.VMEM)
    dma = pltpu.SemaphoreType.DMA
    others = peers - 1
    outs = pl.pallas_call(
        functools.partial(kernel, cfg),
        out_shape=(
            jax.ShapeDtypeStruct((pix, chans), f32),
            jax.ShapeDtypeStruct((pix, chans), f32),
            jax.ShapeDtypeStruct((depth, taps, chans), f32),
            jax.ShapeDtypeStruct((depth, chans), f32),
        ),
        in_specs=[vmem] * 4,
        out_specs=(vmem,) * 4,
        scratch_shapes=[
            pltpu.VMEM((depth + 1, padded, 3 * chans), bf16),
            pltpu.VMEM((2, padded, 3 * chans), bf16),
            pltpu.VMEM((depth, pix, chans), f32),
            pltpu.VMEM((pix, chans), f32),
            pltpu.VMEM((pix, chans), bf16),
            pltpu.VMEM((pix, chans), bf16),
            pltpu.VMEM((pix, chans), bf16),
            pltpu.VMEM((pix, chans), bf16),
            pltpu.VMEM((depth, taps, chans), bf16),
            pltpu.VMEM((depth, 3 * chans, pix), bf16),
            pltpu.VMEM((depth, 1, chans), f32),
            pltpu.VMEM((groups, group_rows, chans), bf16),
            pltpu.VMEM((groups, others, share, chans), bf16),
            pltpu.VMEM((groups, group_rows, chans), bf16),
            pltpu.VMEM((peers, -(-depth // 8) * 8, chans), f32),
            dma((bands,)), dma((bands,)), dma((bands,)), dma((bands,)),
            dma((groups, others)), dma((groups, others)),
            dma((groups, others)), dma((groups, others)),
            dma((others,)), dma((others,)),
        ],
        compiler_params=pltpu.CompilerParams(
            collective_id=0, has_side_effects=True, vmem_limit_bytes=56 * 1024 * 1024
        ),
    )(
        starts.reshape(pix, chans), weights.reshape(depth, taps, chans), biases,
        adj_ends.reshape(pix, chans),
    )
    ends, adj_starts, wgrad, bgrad = outs
    return (
        ends.reshape(starts.shape), adj_starts.reshape(starts.shape),
        wgrad.reshape(weights.shape), bgrad,
    )


def solution(mesh):
    in_specs = (
        P("layer", "dp", None, None, None),
        P("layer", None, None, None),
        P("layer", None),
        P("layer", "dp", None, None, None),
    )
    out_specs = (
        P("layer", "dp", None, None, None),
        P("layer", "dp", None, None, None),
        P("layer", None, None, None),
        P("layer", None),
    )
    run = functools.partial(local, mesh.shape["layer"], mesh.shape["dp"])
    return jax.shard_map(run, mesh=mesh, in_specs=in_specs, out_specs=out_specs, check_vma=False)
```

```python
import functools
import math

import jax
import jax.numpy as jnp
from jax import lax
from jax.experimental import pallas as pl
from jax.experimental.pallas import tpu as pltpu
from jax.sharding import PartitionSpec as P

step_size = 0.25
MESH = pl.DeviceIdType.MESH
f32 = jnp.float32
bf16 = jnp.bfloat16


def kernel(
    cfg,
    starts, weights, biases, adj_ends,
    ends_out, adj_out, wgrad_out, bgrad,
    ends, adj_starts, a3f, a3s, slope, offs, ent, ext, txf, txb, wt, a3t, brow,
    gsend, rx1, mid, rx2, gred, bias_all,
    fsend, frecv, bsend, brecv, one_send, one_recv, two_send, two_recv,
    three_send, three_recv, four_send, four_recv, bi_send, bi_recv, out_sem,
):
    blocks, peers, lows, depth, side, chans, groups, bands, chunk = cfg
    highs = peers // lows
    pix = side * side
    pad = side
    taps = 9 * chans
    per_group = depth // groups
    group_rows = per_group * taps
    half = group_rows // 2
    share = half // peers
    coarse_step = depth * step_size
    grad_scale = 1.0 / (side * math.sqrt(peers))
    band = pix // bands

    k = lax.axis_index("layer")
    me = lax.axis_index("dp")
    first = k == 0
    last = k == blocks - 1
    peer = [lax.rem(me + d, peers) for d in range(1, peers)]

    barrier = pltpu.get_barrier_semaphore()

    @pl.when(jnp.logical_not(first))
    def _():
        pl.semaphore_signal(barrier, inc=1, device_id={"layer": k - 1}, device_id_type=MESH)

    @pl.when(jnp.logical_not(last))
    def _():
        pl.semaphore_signal(barrier, inc=1, device_id={"layer": k + 1}, device_id_type=MESH)

    for p in peer:
        pl.semaphore_signal(barrier, inc=1, device_id={"dp": p}, device_id_type=MESH)
    greeted = (peers - 1) + jnp.where(first, 0, 1) + jnp.where(last, 0, 1)

    def put3(dst, row, val):
        rows = val.shape[0]
        col = lax.rem(lax.broadcasted_iota(jnp.int32, (rows, chans), 0), side)
        before = jnp.where(col == 0, 0.0, pltpu.roll(val, 1, 0))
        after = jnp.where(col == side - 1, 0.0, pltpu.roll(val, rows - 1, 0))
        at = pl.ds(pad + row, rows)
        dst[at, 0:chans] = before.astype(bf16)
        dst[at, chans : 2 * chans] = val.astype(bf16)
        dst[at, 2 * chans : 3 * chans] = after.astype(bf16)

    def conv(src, row, rows, mat):
        lhs = jnp.concatenate([src[pl.ds(row + e * side, rows), :] for e in range(3)], axis=1)
        return jnp.dot(lhs, mat, preferred_element_type=f32)

    bias32 = biases[...].astype(f32)
    for i in range(depth):
        brow[i] = bias32[i : i + 1]
    zeros = jnp.zeros((pad, 3 * chans), bf16)
    for i in range(depth + 1):
        a3f[i, 0:pad] = zeros
        a3f[i, pad + pix : 2 * pad + pix] = zeros
    for i in range(2):
        a3s[i, 0:pad] = zeros
        a3s[i, pad + pix : 2 * pad + pix] = zeros

    chunks = list(range(0, pix, chunk))

    for r in chunks:
        put3(a3f.at[0], r, starts[r : r + chunk])
    for r in chunks:
        act = jnp.tanh(conv(a3f.at[0], r, chunk, weights[0]) + brow[0])
        slope[0, r : r + chunk] = 1.0 - act * act
        u0 = starts[r : r + chunk]
        u1 = u0 + step_size * act
        offs[r : r + chunk] = u0 + coarse_step * act
        ends[r : r + chunk] = u1
        put3(a3f.at[1], r, u1)

    def forward_layer(i, _):
        for r in chunks:
            act = jnp.tanh(conv(a3f.at[i], r, chunk, weights[i]) + brow[i])
            slope[i, r : r + chunk] = 1.0 - act * act
            u = ends[r : r + chunk] + step_size * act
            ends[r : r + chunk] = u
            put3(a3f.at[i + 1], r, u)
        return 0

    lax.fori_loop(1, depth, forward_layer, 0)
    for r in chunks:
        offs[r : r + chunk] = ends[r : r + chunk] - offs[r : r + chunk]

    def turn_weights():
        def one(i, _):
            for t in range(9):
                wt[i, t * chans : (t + 1) * chans] = weights[i, (8 - t) * chans : (9 - t) * chans].T
            return 0

        lax.fori_loop(0, depth, one, 0)

    def turn_states():
        def one(i, _):
            for d in range(3):
                for r in range(0, pix, chans):
                    a3t[i, d * chans : (d + 1) * chans, r : r + chans] = a3f[
                        i, pad + r : pad + r + chans, d * chans : (d + 1) * chans
                    ].T
            return 0

        lax.fori_loop(0, depth, one, 0)

    early = k < blocks // 2
    late = jnp.logical_not(early)
    pl.when(late)(turn_weights)

    pl.semaphore_wait(barrier, greeted)

    def hop(src, dst, send, recv, b, to):
        at = pl.ds(b * band, band)
        return pltpu.make_async_remote_copy(
            src_ref=src.at[at], dst_ref=dst.at[at], send_sem=send.at[b], recv_sem=recv.at[b],
            device_id={"layer": to}, device_id_type=MESH,
        )

    up = lax.rem(k + 1, blocks)
    down = lax.rem(k + blocks - 1, blocks)
    fwd = [hop(txf, ent, fsend, frecv, b, up) for b in range(bands)]
    bwd = [hop(txb, ext, bsend, brecv, b, down) for b in range(bands)]

    @pl.when(first)
    def _():
        for b in range(bands):
            at = pl.ds(b * band, band)
            txf[at] = ends[at].astype(bf16)
            fwd[b].start()

    @pl.when(jnp.logical_not(first))
    def _():
        def work(b):
            at = pl.ds(b * band, band)
            act = jnp.tanh(conv(a3f.at[0], b * band, band, weights[0]) + brow[0])
            state = ent[at].astype(f32)

            @pl.when(jnp.logical_not(last))
            def _():
                txf[at] = (offs[at] + (state + coarse_step * act)).astype(bf16)
                fwd[b].start()

            slope[0, at] = 1.0 - act * act
            u = state + step_size * act
            ends[at] = u
            put3(a3f.at[1], b * band, u)

        for b in range(bands):
            fwd[b].wait_recv()
            put3(a3f.at[0], b * band, ent[pl.ds(b * band, band)].astype(f32))
            if b:
                work(b - 1)
        work(bands - 1)
        lax.fori_loop(1, depth, forward_layer, 0)

    ends_copy = pltpu.make_async_copy(ends, ends_out, out_sem.at[0])
    ends_copy.start()
    pl.when(early)(turn_weights)

    top = depth - 1
    for r in chunks:
        l = adj_ends[r : r + chunk]
        adj_starts[r : r + chunk] = l
        put3(a3s.at[top % 2], r, slope[top, r : r + chunk] * l)

    def adjoint_layer(i):
        now = lax.rem(i, 2)
        below = jnp.maximum(i - 1, 0)
        for r in chunks:
            l = adj_starts[r : r + chunk] + step_size * conv(a3s.at[now], r, chunk, wt[i])
            adj_starts[r : r + chunk] = l
            put3(a3s.at[1 - now], r, slope[below, r : r + chunk] * l)

    def back_layer(j, _):
        adjoint_layer(top - j)
        return 0

    lax.fori_loop(0, depth, back_layer, 0)

    @pl.when(last)
    def _():
        for b in range(bands):
            at = pl.ds(b * band, band)
            txb[at] = adj_starts[at].astype(bf16)
            bwd[b].start()

    pl.when(early)(turn_states)

    @pl.when(jnp.logical_not(last))
    def _():
        @pl.when(jnp.logical_not(first))
        def _():
            def work(b):
                at = pl.ds(b * band, band)
                diff = ext[at].astype(f32) - adj_ends[at]
                out = adj_starts[at] + (diff + coarse_step * conv(a3s.at[0], b * band, band, wt[0]))
                txb[at] = out.astype(bf16)
                bwd[b].start()

            for b in range(bands):
                at = pl.ds(b * band, band)
                bwd[b].wait_recv()
                put3(a3s.at[0], b * band, slope[0, at] * (ext[at].astype(f32) - adj_ends[at]))
                if b:
                    work(b - 1)
            work(bands - 1)

        @pl.when(first)
        def _():
            for b in range(bands):
                bwd[b].wait_recv()

        for r in chunks:
            adj_starts[r : r + chunk] = ext[r : r + chunk].astype(f32)

    @pl.when(last)
    def _():
        for r in chunks:
            adj_starts[r : r + chunk] = adj_ends[r : r + chunk]

    for r in chunks:
        put3(a3s.at[top % 2], r, slope[top, r : r + chunk] * adj_starts[r : r + chunk])
    pl.when(late)(turn_states)

    high, low = me // lows, lax.rem(me, lows)
    counts = ((lows, highs), (highs, lows))
    spots = ((low, high), (high, low))

    def turned(h, stage, d):
        c = list(spots[h])
        c[stage] = lax.rem(c[stage] + d + 1, counts[h][stage])
        return c

    def number(h, c):
        return c[1] * lows + c[0] if h == 0 else c[0] * lows + c[1]

    def wide(h, c):
        rows = half // counts[h][0]
        return pl.ds(pl.multiple_of(h * half + c[0] * rows, 16), rows)

    def narrow(h, c):
        rows = half // counts[h][0]
        return pl.ds(pl.multiple_of(h * half + c[0] * rows + c[1] * share, 16), share)

    def send(src, dst, ssem, rsem, to):
        return pltpu.make_async_remote_copy(
            src_ref=src, dst_ref=dst, send_sem=ssem, recv_sem=rsem,
            device_id={"dp": to}, device_id_type=MESH,
        )

    def one(g, h):
        rows = pl.ds(0, half // counts[h][0])
        for d in range(counts[h][0] - 1):
            c = turned(h, 0, d)
            yield send(gsend.at[g, wide(h, c)], rx1.at[g, h, d, rows],
                       one_send.at[g, h, d], one_recv.at[g, h, d], number(h, c))

    def two(g, h):
        for d in range(counts[h][1] - 1):
            c = turned(h, 1, d)
            src = pl.ds(pl.multiple_of(c[1] * share, 16), share)
            yield send(mid.at[g, h, src], rx2.at[g, h, d],
                       two_send.at[g, h, d], two_recv.at[g, h, d], number(h, c))

    def three(g, h):
        at = narrow(h, spots[h])
        for d in range(counts[h][1] - 1):
            yield send(gred.at[g, at], gred.at[g, at],
                       three_send.at[g, h, d], three_recv.at[g, h, d], number(h, turned(h, 1, d)))

    def four(g, h):
        at = wide(h, spots[h])
        for d in range(counts[h][0] - 1):
            yield send(gred.at[g, at], gred.at[g, at],
                       four_send.at[g, h, d], four_recv.at[g, h, d], number(h, turned(h, 0, d)))

    def start_one(g):
        for h in range(2):
            for c in one(g, h):
                c.start()

    def start_two(g):
        for h in range(2):
            for c in one(g, h):
                c.wait_recv()
            rows = half // counts[h][0]
            total = gsend[g, wide(h, spots[h])].astype(f32)
            for d in range(counts[h][0] - 1):
                total = total + rx1[g, h, d, 0:rows].astype(f32)
            mid[g, h, 0:rows] = total.astype(bf16)
            for c in two(g, h):
                c.start()

    def start_three(g):
        for h in range(2):
            for c in two(g, h):
                c.wait_recv()
            own = pl.ds(pl.multiple_of(spots[h][1] * share, 16), share)
            total = mid[g, h, own].astype(f32)
            for d in range(counts[h][1] - 1):
                total = total + rx2[g, h, d].astype(f32)
            gred[g, narrow(h, spots[h])] = total.astype(bf16)
            for c in three(g, h):
                c.start()

    def start_four(g):
        for h in range(2):
            for c in three(g, h):
                c.wait_recv()
            for c in four(g, h):
                c.start()

    def bias_copy(d):
        return pltpu.make_async_remote_copy(
            src_ref=bias_all.at[me], dst_ref=bias_all.at[me],
            send_sem=bi_send.at[d], recv_sem=bi_recv.at[d],
            device_id={"dp": peer[d]}, device_id_type=MESH,
        )

    def final_group(j, _):
        g = groups - 1 - j
        for q in reversed(range(per_group)):
            i = g * per_group + q
            now = lax.rem(i, 2)
            sig = a3s.at[now]
            rhs = jnp.concatenate(
                [sig[(2 - e) * side : (2 - e) * side + pix, chans : 2 * chans] for e in range(3)], axis=1
            )
            found = jnp.dot(a3t[i], rhs, preferred_element_type=f32) * grad_scale
            for e in range(3):
                for d in range(3):
                    to = q * taps + (3 * e + d) * chans
                    gsend[g, to : to + chans] = found[
                        d * chans : (d + 1) * chans, e * chans : (e + 1) * chans
                    ].astype(bf16)
            summed = jnp.sum(sig[pad : pad + pix, chans : 2 * chans].astype(f32), axis=0, keepdims=True)
            brow[i] = summed * grad_scale
            if q == 0:
                start_one(g)
            adjoint_layer(i)

        for lag, stage in ((3, start_four), (2, start_three), (1, start_two)):
            @pl.when(j >= lag)
            def _():
                stage(jnp.minimum(g + lag, groups - 1))

        return 0

    lax.fori_loop(0, groups, final_group, 0)
    for i in range(depth):
        bias_all[me, i : i + 1] = brow[i]
    adj_copy = pltpu.make_async_copy(adj_starts, adj_out, out_sem.at[1])
    adj_copy.start()
    for d in range(peers - 1):
        bias_copy(d).start()
    for step in range(3):
        for lag, stage in ((3, start_four), (2, start_three), (1, start_two)):
            j = groups + step - lag
            if 0 <= j < groups:
                stage(groups - 1 - j)

    for d in range(peers - 1):
        bias_copy(d).wait_recv()
    total = bias_all[0, 0:depth]
    for p in range(1, peers):
        total = total + bias_all[p, 0:depth]
    bgrad[...] = total

    def grad_copy(g):
        return pltpu.make_async_copy(gred.at[g], wgrad_out.at[g], out_sem.at[2 + g])

    def finish(j, _):
        g = groups - 1 - j
        for h in range(2):
            for c in four(g, h):
                c.wait_recv()
        grad_copy(g).start()
        return 0

    lax.fori_loop(0, groups, finish, 0)

    @pl.when(jnp.logical_not(last))
    def _():
        for b in range(bands):
            fwd[b].wait_send()

    @pl.when(jnp.logical_not(first))
    def _():
        for b in range(bands):
            bwd[b].wait_send()

    def drain(g, _):
        for h in range(2):
            for stage in (one, two, three, four):
                for c in stage(g, h):
                    c.wait_send()
        grad_copy(g).wait()
        return 0

    lax.fori_loop(0, groups, drain, 0)
    for d in range(peers - 1):
        bias_copy(d).wait_send()
    ends_copy.wait()
    adj_copy.wait()


def unpack(ends, adj_starts, wgrad, bgrad, ends_out, adj_out, wgrad_out, bgrad_out):
    ends_out[...] = ends[...]
    adj_out[...] = adj_starts[...]
    wgrad_out[...] = wgrad[...].astype(f32)
    bgrad_out[...] = bgrad[...]


def local(blocks, peers, starts, weights, biases, adj_ends):
    _, _, side, _, chans = starts.shape
    depth = weights.shape[0]
    pix = side * side
    taps = 9 * chans
    bands = 8
    chunk = min(256, pix)
    lows = min(n for n in range(1, peers + 1) if peers % n == 0 and n * n >= peers)
    highs = peers // lows
    groups = max(
        g for g in range(1, depth + 1)
        if depth % g == 0 and (depth // g * taps) % (32 * peers) == 0
    )
    group_rows = depth // groups * taps
    half = group_rows // 2
    slots = max(1, lows - 1, highs - 1)
    cfg = (blocks, peers, lows, depth, side, chans, groups, bands, chunk)
    padded = pix + 2 * side
    vmem = pl.BlockSpec(memory_space=pltpu.VMEM)
    anywhere = pl.BlockSpec(memory_space=pl.ANY)
    dma = pltpu.SemaphoreType.DMA
    others = peers - 1
    outs = pl.pallas_call(
        functools.partial(kernel, cfg),
        out_shape=(
            jax.ShapeDtypeStruct((pix, chans), f32),
            jax.ShapeDtypeStruct((pix, chans), f32),
            jax.ShapeDtypeStruct((groups, group_rows, chans), bf16),
            jax.ShapeDtypeStruct((depth, chans), f32),
        ),
        in_specs=[vmem] * 4,
        out_specs=(anywhere, anywhere, anywhere, vmem),
        scratch_shapes=[
            pltpu.VMEM((pix, chans), f32),
            pltpu.VMEM((pix, chans), f32),
            pltpu.VMEM((depth + 1, padded, 3 * chans), bf16),
            pltpu.VMEM((2, padded, 3 * chans), bf16),
            pltpu.VMEM((depth, pix, chans), f32),
            pltpu.VMEM((pix, chans), f32),
            pltpu.VMEM((pix, chans), bf16),
            pltpu.VMEM((pix, chans), bf16),
            pltpu.VMEM((pix, chans), bf16),
            pltpu.VMEM((pix, chans), bf16),
            pltpu.VMEM((depth, taps, chans), bf16),
            pltpu.VMEM((depth, 3 * chans, pix), bf16),
            pltpu.VMEM((depth, 1, chans), f32),
            pltpu.VMEM((groups, group_rows, chans), bf16),
            pltpu.VMEM((groups, 2, slots, half // min(lows, highs), chans), bf16),
            pltpu.VMEM((groups, 2, half // min(lows, highs), chans), bf16),
            pltpu.VMEM((groups, 2, slots, half // peers, chans), bf16),
            pltpu.VMEM((groups, group_rows, chans), bf16),
            pltpu.VMEM((peers, -(-depth // 8) * 8, chans), f32),
            dma((bands,)), dma((bands,)), dma((bands,)), dma((bands,)),
            *[dma((groups, 2, slots))] * 8,
            dma((max(1, others),)), dma((max(1, others),)),
            dma((2 + groups,)),
        ],
        compiler_params=pltpu.CompilerParams(
            collective_id=0, has_side_effects=True, vmem_limit_bytes=56 * 1024 * 1024
        ),
    )(
        starts.reshape(pix, chans), weights.reshape(depth, taps, chans), biases,
        adj_ends.reshape(pix, chans),
    )
    rows = pix // groups
    part = pl.BlockSpec((rows, chans), lambda g: (g, 0))
    block = pl.BlockSpec((1, group_rows, chans), lambda g: (g, 0, 0))
    whole = pl.BlockSpec((depth, chans), lambda g: (0, 0))
    specs = (part, part, block, whole)
    ends, adj_starts, wgrad, bgrad = pl.pallas_call(
        unpack,
        grid=(groups,),
        out_shape=tuple(jax.ShapeDtypeStruct(o.shape, f32) for o in outs),
        in_specs=list(specs),
        out_specs=specs,
        compiler_params=pltpu.CompilerParams(vmem_limit_bytes=32 * 1024 * 1024),
    )(*outs)
    return (
        ends.reshape(starts.shape), adj_starts.reshape(starts.shape),
        wgrad.reshape(weights.shape), bgrad,
    )


def solution(mesh):
    in_specs = (
        P("layer", "dp", None, None, None),
        P("layer", None, None, None),
        P("layer", None),
        P("layer", "dp", None, None, None),
    )
    out_specs = (
        P("layer", "dp", None, None, None),
        P("layer", "dp", None, None, None),
        P("layer", None, None, None),
        P("layer", None),
    )
    run = functools.partial(local, mesh.shape["layer"], mesh.shape["dp"])
    return jax.shard_map(run, mesh=mesh, in_specs=in_specs, out_specs=out_specs, check_vma=False)
```

```python
import functools
import math

import jax
import jax.numpy as jnp
from jax import lax
from jax.experimental import pallas as pl
from jax.experimental.pallas import tpu as pltpu
from jax.sharding import PartitionSpec as P

step_size = 0.25
MESH = pl.DeviceIdType.MESH
f32 = jnp.float32
bf16 = jnp.bfloat16


def kernel(
    cfg,
    starts, weights, biases, adj_ends,
    ends_out, adj_out, wgrad_out, bgrad,
    ends, adj_starts, a3f, a3s, slope, offs, ent, ext, txf, txb, wt, a3t, brow,
    gsend, rx1, mid, rx2, gred, bias_all,
    fsend, frecv, bsend, brecv, one_send, one_recv, two_send, two_recv,
    three_send, three_recv, four_send, four_recv, bi_send, bi_recv, out_sem,
):
    blocks, peers, lows, depth, side, chans, groups, bands, chunk = cfg
    highs = peers // lows
    pix = side * side
    pad = side
    taps = 9 * chans
    per_group = depth // groups
    group_rows = per_group * taps
    half = group_rows // 2
    share = half // peers
    top = depth - 1
    coarse_step = depth * step_size
    grad_scale = 1.0 / (side * math.sqrt(peers))
    band = pix // bands

    k = lax.axis_index("layer")
    me = lax.axis_index("dp")
    first = k == 0
    last = k == blocks - 1
    peer = [lax.rem(me + d, peers) for d in range(1, peers)]

    barrier = pltpu.get_barrier_semaphore()

    @pl.when(jnp.logical_not(first))
    def _():
        pl.semaphore_signal(barrier, inc=1, device_id={"layer": k - 1}, device_id_type=MESH)

    @pl.when(jnp.logical_not(last))
    def _():
        pl.semaphore_signal(barrier, inc=1, device_id={"layer": k + 1}, device_id_type=MESH)

    for p in peer:
        pl.semaphore_signal(barrier, inc=1, device_id={"dp": p}, device_id_type=MESH)
    greeted = (peers - 1) + jnp.where(first, 0, 1) + jnp.where(last, 0, 1)

    def put3(dst, row, val):
        rows = val.shape[0]
        col = lax.rem(lax.broadcasted_iota(jnp.int32, (rows, chans), 0), side)
        before = jnp.where(col == 0, 0.0, pltpu.roll(val, 1, 0))
        after = jnp.where(col == side - 1, 0.0, pltpu.roll(val, rows - 1, 0))
        at = pl.ds(pad + row, rows)
        dst[at, 0:chans] = before.astype(bf16)
        dst[at, chans : 2 * chans] = val.astype(bf16)
        dst[at, 2 * chans : 3 * chans] = after.astype(bf16)

    def conv(src, row, rows, mat):
        lhs = jnp.concatenate([src[pl.ds(row + e * side, rows), :] for e in range(3)], axis=1)
        return jnp.dot(lhs, mat, preferred_element_type=f32)

    bias32 = biases[...].astype(f32)
    for i in range(depth):
        brow[i] = bias32[i : i + 1]
    zeros = jnp.zeros((pad, 3 * chans), bf16)
    for i in range(depth):
        a3f[i, 0:pad] = zeros
        a3f[i, pad + pix : 2 * pad + pix] = zeros
    for i in range(2):
        a3s[i, 0:pad] = zeros
        a3s[i, pad + pix : 2 * pad + pix] = zeros

    chunks = list(range(0, pix, chunk))

    for r in chunks:
        put3(a3f.at[0], r, starts[r : r + chunk])
    for r in chunks:
        act = jnp.tanh(conv(a3f.at[0], r, chunk, weights[0]) + brow[0])
        slope[0, r : r + chunk] = 1.0 - act * act
        u0 = starts[r : r + chunk]
        u1 = u0 + step_size * act
        offs[r : r + chunk] = u0 + coarse_step * act
        ends[r : r + chunk] = u1
        if top:
            put3(a3f.at[1], r, u1)

    def forward_layer(i):
        for r in chunks:
            act = jnp.tanh(conv(a3f.at[i], r, chunk, weights[i]) + brow[i])
            slope[i, r : r + chunk] = 1.0 - act * act
            u = ends[r : r + chunk] + step_size * act
            ends[r : r + chunk] = u
            if i < top:
                put3(a3f.at[i + 1], r, u)

    for i in range(1, depth):
        forward_layer(i)
    for r in chunks:
        offs[r : r + chunk] = ends[r : r + chunk] - offs[r : r + chunk]

    def turn_weights():
        def one(i, _):
            for t in range(9):
                wt[i, t * chans : (t + 1) * chans] = weights[i, (8 - t) * chans : (9 - t) * chans].T
            return 0

        lax.fori_loop(0, depth, one, 0)

    def turn_states():
        def one(i, _):
            for d in range(3):
                for r in range(0, pix, chans):
                    a3t[i, d * chans : (d + 1) * chans, r : r + chans] = a3f[
                        i, pad + r : pad + r + chans, d * chans : (d + 1) * chans
                    ].T
            return 0

        lax.fori_loop(0, depth, one, 0)

    early = k < blocks // 2
    late = jnp.logical_not(early)
    pl.when(late)(turn_weights)

    pl.semaphore_wait(barrier, greeted)

    def hop(src, dst, send, recv, b, to):
        at = pl.ds(b * band, band)
        return pltpu.make_async_remote_copy(
            src_ref=src.at[at], dst_ref=dst.at[at], send_sem=send.at[b], recv_sem=recv.at[b],
            device_id={"layer": to}, device_id_type=MESH,
        )

    up = lax.rem(k + 1, blocks)
    down = lax.rem(k + blocks - 1, blocks)
    fwd = [hop(txf, ent, fsend, frecv, b, up) for b in range(bands)]
    bwd = [hop(txb, ext, bsend, brecv, b, down) for b in range(bands)]

    @pl.when(first)
    def _():
        for b in range(bands):
            at = pl.ds(b * band, band)
            txf[at] = ends[at].astype(bf16)
            fwd[b].start()

    @pl.when(jnp.logical_not(first))
    def _():
        def work(b):
            at = pl.ds(b * band, band)
            act = jnp.tanh(conv(a3f.at[0], b * band, band, weights[0]) + brow[0])
            state = ent[at].astype(f32)

            @pl.when(jnp.logical_not(last))
            def _():
                txf[at] = (offs[at] + (state + coarse_step * act)).astype(bf16)
                fwd[b].start()

            slope[0, at] = 1.0 - act * act
            u = state + step_size * act
            ends[at] = u
            if top:
                put3(a3f.at[1], b * band, u)

        for b in range(bands):
            fwd[b].wait_recv()
            put3(a3f.at[0], b * band, ent[pl.ds(b * band, band)].astype(f32))
            if b:
                work(b - 1)
        work(bands - 1)
        for i in range(1, depth):
            forward_layer(i)

    ends_copy = pltpu.make_async_copy(ends, ends_out, out_sem.at[0])
    ends_copy.start()
    pl.when(early)(turn_weights)

    for r in chunks:
        l = adj_ends[r : r + chunk]
        adj_starts[r : r + chunk] = l
        put3(a3s.at[top % 2], r, slope[top, r : r + chunk] * l)

    def adjoint_layer(i):
        now = i % 2
        for r in chunks:
            l = adj_starts[r : r + chunk] + step_size * conv(a3s.at[now], r, chunk, wt[i])
            adj_starts[r : r + chunk] = l
            if i:
                put3(a3s.at[1 - now], r, slope[i - 1, r : r + chunk] * l)

    for i in reversed(range(depth)):
        adjoint_layer(i)

    @pl.when(last)
    def _():
        for b in range(bands):
            at = pl.ds(b * band, band)
            txb[at] = adj_starts[at].astype(bf16)
            bwd[b].start()

    pl.when(early)(turn_states)

    @pl.when(jnp.logical_not(last))
    def _():
        @pl.when(jnp.logical_not(first))
        def _():
            def work(b):
                at = pl.ds(b * band, band)
                diff = ext[at].astype(f32) - adj_ends[at]
                out = adj_starts[at] + (diff + coarse_step * conv(a3s.at[0], b * band, band, wt[0]))
                txb[at] = out.astype(bf16)
                bwd[b].start()

            for b in range(bands):
                at = pl.ds(b * band, band)
                bwd[b].wait_recv()
                put3(a3s.at[0], b * band, slope[0, at] * (ext[at].astype(f32) - adj_ends[at]))
                if b:
                    work(b - 1)
            work(bands - 1)

        @pl.when(first)
        def _():
            for b in range(bands):
                bwd[b].wait_recv()

        for r in chunks:
            adj_starts[r : r + chunk] = ext[r : r + chunk].astype(f32)

    @pl.when(last)
    def _():
        for r in chunks:
            adj_starts[r : r + chunk] = adj_ends[r : r + chunk]

    for r in chunks:
        put3(a3s.at[top % 2], r, slope[top, r : r + chunk] * adj_starts[r : r + chunk])
    pl.when(late)(turn_states)

    high, low = me // lows, lax.rem(me, lows)
    counts = ((lows, highs), (highs, lows))
    spots = ((low, high), (high, low))

    def turned(h, stage, d):
        c = list(spots[h])
        c[stage] = lax.rem(c[stage] + d + 1, counts[h][stage])
        return c

    def number(h, c):
        return c[1] * lows + c[0] if h == 0 else c[0] * lows + c[1]

    def wide(h, c):
        rows = half // counts[h][0]
        return pl.ds(pl.multiple_of(h * half + c[0] * rows, 16), rows)

    def narrow(h, c):
        rows = half // counts[h][0]
        return pl.ds(pl.multiple_of(h * half + c[0] * rows + c[1] * share, 16), share)

    def send(src, dst, ssem, rsem, to):
        return pltpu.make_async_remote_copy(
            src_ref=src, dst_ref=dst, send_sem=ssem, recv_sem=rsem,
            device_id={"dp": to}, device_id_type=MESH,
        )

    def one(g, h):
        rows = pl.ds(0, half // counts[h][0])
        for d in range(counts[h][0] - 1):
            c = turned(h, 0, d)
            yield send(gsend.at[g, wide(h, c)], rx1.at[g, h, d, rows],
                       one_send.at[g, h, d], one_recv.at[g, h, d], number(h, c))

    def two(g, h):
        for d in range(counts[h][1] - 1):
            c = turned(h, 1, d)
            src = pl.ds(pl.multiple_of(c[1] * share, 16), share)
            yield send(mid.at[g, h, src], rx2.at[g, h, d],
                       two_send.at[g, h, d], two_recv.at[g, h, d], number(h, c))

    def three(g, h):
        at = narrow(h, spots[h])
        for d in range(counts[h][1] - 1):
            yield send(gred.at[g, at], gred.at[g, at],
                       three_send.at[g, h, d], three_recv.at[g, h, d], number(h, turned(h, 1, d)))

    def four(g, h):
        at = wide(h, spots[h])
        for d in range(counts[h][0] - 1):
            yield send(gred.at[g, at], gred.at[g, at],
                       four_send.at[g, h, d], four_recv.at[g, h, d], number(h, turned(h, 0, d)))

    def start_one(g):
        for h in range(2):
            for c in one(g, h):
                c.start()

    def start_two(g):
        for h in range(2):
            for c in one(g, h):
                c.wait_recv()
            rows = half // counts[h][0]
            total = gsend[g, wide(h, spots[h])].astype(f32)
            for d in range(counts[h][0] - 1):
                total = total + rx1[g, h, d, 0:rows].astype(f32)
            mid[g, h, 0:rows] = total.astype(bf16)
            for c in two(g, h):
                c.start()

    def start_three(g):
        for h in range(2):
            for c in two(g, h):
                c.wait_recv()
            own = pl.ds(pl.multiple_of(spots[h][1] * share, 16), share)
            total = mid[g, h, own].astype(f32)
            for d in range(counts[h][1] - 1):
                total = total + rx2[g, h, d].astype(f32)
            gred[g, narrow(h, spots[h])] = total.astype(bf16)
            for c in three(g, h):
                c.start()

    def start_four(g):
        for h in range(2):
            for c in three(g, h):
                c.wait_recv()
            for c in four(g, h):
                c.start()

    def bias_copy(d):
        return pltpu.make_async_remote_copy(
            src_ref=bias_all.at[me], dst_ref=bias_all.at[me],
            send_sem=bi_send.at[d], recv_sem=bi_recv.at[d],
            device_id={"dp": peer[d]}, device_id_type=MESH,
        )

    for j in range(groups):
        g = groups - 1 - j
        for q in reversed(range(per_group)):
            i = g * per_group + q
            sig = a3s.at[i % 2]
            rhs = jnp.concatenate(
                [sig[(2 - e) * side : (2 - e) * side + pix, chans : 2 * chans] for e in range(3)], axis=1
            )
            found = jnp.dot(a3t[i], rhs, preferred_element_type=f32) * grad_scale
            for e in range(3):
                for d in range(3):
                    to = q * taps + (3 * e + d) * chans
                    gsend[g, to : to + chans] = found[
                        d * chans : (d + 1) * chans, e * chans : (e + 1) * chans
                    ].astype(bf16)
            summed = jnp.sum(sig[pad : pad + pix, chans : 2 * chans].astype(f32), axis=0, keepdims=True)
            brow[i] = summed * grad_scale
            if q == 0:
                start_one(g)
            adjoint_layer(i)

        for lag, stage in ((3, start_four), (2, start_three), (1, start_two)):
            if j >= lag:
                stage(g + lag)

    for i in range(depth):
        bias_all[me, i : i + 1] = brow[i]
    adj_copy = pltpu.make_async_copy(adj_starts, adj_out, out_sem.at[1])
    adj_copy.start()
    for d in range(peers - 1):
        bias_copy(d).start()
    for step in range(3):
        for lag, stage in ((3, start_four), (2, start_three), (1, start_two)):
            j = groups + step - lag
            if 0 <= j < groups:
                stage(groups - 1 - j)

    for d in range(peers - 1):
        bias_copy(d).wait_recv()
    total = bias_all[0, 0:depth]
    for p in range(1, peers):
        total = total + bias_all[p, 0:depth]
    bgrad[...] = total

    def grad_copy(g):
        return pltpu.make_async_copy(gred.at[g], wgrad_out.at[g], out_sem.at[2 + g])

    def finish(j, _):
        g = groups - 1 - j
        for h in range(2):
            for c in four(g, h):
                c.wait_recv()
        grad_copy(g).start()
        return 0

    lax.fori_loop(0, groups, finish, 0)

    @pl.when(jnp.logical_not(last))
    def _():
        for b in range(bands):
            fwd[b].wait_send()

    @pl.when(jnp.logical_not(first))
    def _():
        for b in range(bands):
            bwd[b].wait_send()

    def drain(g, _):
        for h in range(2):
            for stage in (one, two, three, four):
                for c in stage(g, h):
                    c.wait_send()
        grad_copy(g).wait()
        return 0

    lax.fori_loop(0, groups, drain, 0)
    for d in range(peers - 1):
        bias_copy(d).wait_send()
    ends_copy.wait()
    adj_copy.wait()


def unpack(ends, adj_starts, wgrad, bgrad, ends_out, adj_out, wgrad_out, bgrad_out):
    ends_out[...] = ends[...]
    adj_out[...] = adj_starts[...]
    wgrad_out[...] = wgrad[...].astype(f32)
    bgrad_out[...] = bgrad[...]


def local(blocks, peers, starts, weights, biases, adj_ends):
    _, _, side, _, chans = starts.shape
    depth = weights.shape[0]
    pix = side * side
    taps = 9 * chans
    bands = 8
    chunk = min(256, pix)
    lows = min(n for n in range(1, peers + 1) if peers % n == 0 and n * n >= peers)
    highs = peers // lows
    groups = max(
        g for g in range(1, depth + 1)
        if depth % g == 0 and (depth // g * taps) % (32 * peers) == 0
    )
    group_rows = depth // groups * taps
    half = group_rows // 2
    slots = max(1, lows - 1, highs - 1)
    cfg = (blocks, peers, lows, depth, side, chans, groups, bands, chunk)
    padded = pix + 2 * side
    vmem = pl.BlockSpec(memory_space=pltpu.VMEM)
    anywhere = pl.BlockSpec(memory_space=pl.ANY)
    dma = pltpu.SemaphoreType.DMA
    others = peers - 1
    outs = pl.pallas_call(
        functools.partial(kernel, cfg),
        out_shape=(
            jax.ShapeDtypeStruct((pix, chans), f32),
            jax.ShapeDtypeStruct((pix, chans), f32),
            jax.ShapeDtypeStruct((groups, group_rows, chans), bf16),
            jax.ShapeDtypeStruct((depth, chans), f32),
        ),
        in_specs=[vmem] * 4,
        out_specs=(anywhere, anywhere, anywhere, vmem),
        scratch_shapes=[
            pltpu.VMEM((pix, chans), f32),
            pltpu.VMEM((pix, chans), f32),
            pltpu.VMEM((depth, padded, 3 * chans), bf16),
            pltpu.VMEM((2, padded, 3 * chans), bf16),
            pltpu.VMEM((depth, pix, chans), f32),
            pltpu.VMEM((pix, chans), f32),
            pltpu.VMEM((pix, chans), bf16),
            pltpu.VMEM((pix, chans), bf16),
            pltpu.VMEM((pix, chans), bf16),
            pltpu.VMEM((pix, chans), bf16),
            pltpu.VMEM((depth, taps, chans), bf16),
            pltpu.VMEM((depth, 3 * chans, pix), bf16),
            pltpu.VMEM((depth, 1, chans), f32),
            pltpu.VMEM((groups, group_rows, chans), bf16),
            pltpu.VMEM((groups, 2, slots, half // min(lows, highs), chans), bf16),
            pltpu.VMEM((groups, 2, half // min(lows, highs), chans), bf16),
            pltpu.VMEM((groups, 2, slots, half // peers, chans), bf16),
            pltpu.VMEM((groups, group_rows, chans), bf16),
            pltpu.VMEM((peers, -(-depth // 8) * 8, chans), f32),
            dma((bands,)), dma((bands,)), dma((bands,)), dma((bands,)),
            *[dma((groups, 2, slots))] * 8,
            dma((max(1, others),)), dma((max(1, others),)),
            dma((2 + groups,)),
        ],
        compiler_params=pltpu.CompilerParams(
            collective_id=0, has_side_effects=True, vmem_limit_bytes=56 * 1024 * 1024
        ),
    )(
        starts.reshape(pix, chans), weights.reshape(depth, taps, chans), biases,
        adj_ends.reshape(pix, chans),
    )
    rows = pix // groups
    part = pl.BlockSpec((rows, chans), lambda g: (g, 0))
    block = pl.BlockSpec((1, group_rows, chans), lambda g: (g, 0, 0))
    whole = pl.BlockSpec((depth, chans), lambda g: (0, 0))
    specs = (part, part, block, whole)
    ends, adj_starts, wgrad, bgrad = pl.pallas_call(
        unpack,
        grid=(groups,),
        out_shape=tuple(jax.ShapeDtypeStruct(o.shape, f32) for o in outs),
        in_specs=list(specs),
        out_specs=specs,
        compiler_params=pltpu.CompilerParams(vmem_limit_bytes=60 * 1024 * 1024),
    )(*outs)
    return (
        ends.reshape(starts.shape), adj_starts.reshape(starts.shape),
        wgrad.reshape(weights.shape), bgrad,
    )


def solution(mesh):
    in_specs = (
        P("layer", "dp", None, None, None),
        P("layer", None, None, None),
        P("layer", None),
        P("layer", "dp", None, None, None),
    )
    out_specs = (
        P("layer", "dp", None, None, None),
        P("layer", "dp", None, None, None),
        P("layer", None, None, None),
        P("layer", None),
    )
    run = functools.partial(local, mesh.shape["layer"], mesh.shape["dp"])
    return jax.shard_map(run, mesh=mesh, in_specs=in_specs, out_specs=out_specs, check_vma=False)
```

```python
import functools
import math

import jax
import jax.numpy as jnp
from jax import lax
from jax.experimental import pallas as pl
from jax.experimental.pallas import tpu as pltpu
from jax.sharding import PartitionSpec as P

step_size = 0.25
MESH = pl.DeviceIdType.MESH
f32 = jnp.float32
bf16 = jnp.bfloat16


def kernel(
    cfg,
    starts, weights, biases, adj_ends,
    ends_out, adj_out, wgrad_out, bgrad,
    ends, adj_starts, a3f, a3s, slope, offs, ent, ext, txf, txb, wt, a3t, brow,
    a3c, slope_o, offs_o, rxb, exe, txu, txo, w_o, wt_o, adj_o, bias_o, bias_tx,
    gsend, rx1, mid, rx2, gred, bias_all,
    fsend, frecv, usend, urecv, osend, orecv, bsend, brecv, dsend, drecv, esend, erecv,
    msend, mrecv, one_send, one_recv, two_send, two_recv,
    three_send, three_recv, four_send, four_recv, bi_send, bi_recv, out_sem,
):
    blocks, peers, lows, depth, side, chans, groups, bands, chunk = cfg
    highs = peers // lows
    pix = side * side
    pad = side
    taps = 9 * chans
    per_group = depth // groups
    group_rows = per_group * taps
    half = group_rows // 2
    share = half // peers
    top = depth - 1
    coarse_step = depth * step_size
    grad_scale = 1.0 / (side * math.sqrt(peers))
    band = pix // bands

    k = lax.axis_index("layer")
    me = lax.axis_index("dp")
    first = k == 0
    last = k == blocks - 1
    peer = [lax.rem(me + d, peers) for d in range(1, peers)]

    barrier = pltpu.get_barrier_semaphore()

    even = lax.rem(k, 2) == 0
    odd = lax.rem(k, 2) == 1
    rising = jnp.logical_and(even, k < blocks - 2)
    falling = jnp.logical_and(even, k > 0)
    middle = jnp.logical_and(rising, k > 0)
    crown = k == blocks - 2

    def greet(when, to):
        @pl.when(when)
        def _():
            pl.semaphore_signal(barrier, inc=1, device_id={"layer": to}, device_id_type=MESH)

    greet(even, k + 1)
    greet(odd, k - 1)
    greet(rising, k + 2)
    greet(falling, k - 2)
    for p in peer:
        pl.semaphore_signal(barrier, inc=1, device_id={"dp": p}, device_id_type=MESH)
    greeted = peers + jnp.where(rising, 1, 0) + jnp.where(falling, 1, 0)

    def put3(dst, row, val):
        rows = val.shape[0]
        col = lax.rem(lax.broadcasted_iota(jnp.int32, (rows, chans), 0), side)
        before = jnp.where(col == 0, 0.0, pltpu.roll(val, 1, 0))
        after = jnp.where(col == side - 1, 0.0, pltpu.roll(val, rows - 1, 0))
        at = pl.ds(pad + row, rows)
        dst[at, 0:chans] = before.astype(bf16)
        dst[at, chans : 2 * chans] = val.astype(bf16)
        dst[at, 2 * chans : 3 * chans] = after.astype(bf16)

    def conv(src, row, rows, mat):
        lhs = jnp.concatenate([src[pl.ds(row + e * side, rows), :] for e in range(3)], axis=1)
        return jnp.dot(lhs, mat, preferred_element_type=f32)

    bias32 = biases[...].astype(f32)
    for i in range(depth):
        brow[i] = bias32[i : i + 1]
    zeros = jnp.zeros((pad, 3 * chans), bf16)
    for i in range(depth):
        a3f[i, 0:pad] = zeros
        a3f[i, pad + pix : 2 * pad + pix] = zeros
    for i in range(2):
        a3s[i, 0:pad] = zeros
        a3s[i, pad + pix : 2 * pad + pix] = zeros

    a3c[0:pad] = zeros
    a3c[pad + pix : 2 * pad + pix] = zeros
    bias_tx[...] = jnp.broadcast_to(bias32[0:1], bias_tx.shape)

    chunks = list(range(0, pix, chunk))

    def hop(src, dst, send, recv, b, to):
        at = pl.ds(b * band, band)
        return pltpu.make_async_remote_copy(
            src_ref=src.at[at], dst_ref=dst.at[at], send_sem=send.at[b], recv_sem=recv.at[b],
            device_id={"layer": to}, device_id_type=MESH,
        )

    def to_partner(src, dst, n):
        return pltpu.make_async_remote_copy(
            src_ref=src, dst_ref=dst, send_sem=msend.at[n], recv_sem=mrecv.at[n],
            device_id={"layer": jnp.maximum(k - 1, 0)}, device_id_type=MESH,
        )

    def along(src, dst, send, recv, by):
        to = lax.rem(k + by + blocks, blocks)
        return [hop(src, dst, send, recv, b, to) for b in range(bands)]

    across = along(txf, ent, fsend, frecv, 1)
    upward = along(txu, ent, usend, urecv, 2)
    offset = along(txo, offs_o, osend, orecv, -1)
    handed = along(txb, rxb, bsend, brecv, -1)
    downward = along(txb, ext, dsend, drecv, -2)
    onward = along(ext, ext, esend, erecv, 1)
    lent = [to_partner(weights.at[0], w_o, 0), to_partner(bias_tx, bias_o, 1), to_partner(adj_ends, adj_o, 2)]

    for r in chunks:
        put3(a3f.at[0], r, starts[r : r + chunk])
    for r in chunks:
        act = jnp.tanh(conv(a3f.at[0], r, chunk, weights[0]) + brow[0])
        slope[0, r : r + chunk] = 1.0 - act * act
        u0 = starts[r : r + chunk]
        u1 = u0 + step_size * act
        offs[r : r + chunk] = u0 + coarse_step * act
        ends[r : r + chunk] = u1
        if top:
            put3(a3f.at[1], r, u1)

    pl.semaphore_wait(barrier, greeted)

    @pl.when(odd)
    def _():
        for c in lent:
            c.start()

    def forward_layer(i):
        for r in chunks:
            act = jnp.tanh(conv(a3f.at[i], r, chunk, weights[i]) + brow[i])
            slope[i, r : r + chunk] = 1.0 - act * act
            u = ends[r : r + chunk] + step_size * act
            ends[r : r + chunk] = u
            if i < top:
                put3(a3f.at[i + 1], r, u)

    for i in range(1, depth):
        forward_layer(i)
    for r in chunks:
        offs[r : r + chunk] = ends[r : r + chunk] - offs[r : r + chunk]
        txo[r : r + chunk] = offs[r : r + chunk].astype(bf16)

    @pl.when(odd)
    def _():
        for c in offset:
            c.start()

    @pl.when(even)
    def _():
        for c in lent:
            c.wait_recv()

    def turn_weights():
        def one(i, _):
            for t in range(9):
                wt[i, t * chans : (t + 1) * chans] = weights[i, (8 - t) * chans : (9 - t) * chans].T
            return 0

        lax.fori_loop(0, depth, one, 0)

        @pl.when(even)
        def _():
            for t in range(9):
                wt_o[t * chans : (t + 1) * chans] = w_o[(8 - t) * chans : (9 - t) * chans].T

    def turn_states():
        def one(i, _):
            for d in range(3):
                for r in range(0, pix, chans):
                    a3t[i, d * chans : (d + 1) * chans, r : r + chans] = a3f[
                        i, pad + r : pad + r + chans, d * chans : (d + 1) * chans
                    ].T
            return 0

        lax.fori_loop(0, depth, one, 0)

    early = k < blocks // 2
    late = jnp.logical_not(early)
    pl.when(late)(turn_weights)

    def rows_of(b):
        return pl.ds(b * band, band)

    def enter(b, copies):
        copies[b].wait_recv()
        put3(a3f.at[0], b * band, ent[rows_of(b)].astype(f32))

    def own_step(b, passes):
        at = rows_of(b)
        act = jnp.tanh(conv(a3f.at[0], b * band, band, weights[0]) + brow[0])
        state = ent[at].astype(f32)
        if passes:
            after = offs[at] + (state + coarse_step * act)
            txf[at] = after.astype(bf16)
            put3(a3c, b * band, after)
            across[b].start()
        slope[0, at] = 1.0 - act * act
        u = state + step_size * act
        ends[at] = u
        if top:
            put3(a3f.at[1], b * band, u)

    def pair_step(b):
        at = rows_of(b)
        offset[b].wait_recv()
        act = jnp.tanh(conv(a3c, b * band, band, w_o[...]) + bias_o[0:1])
        after = offs_o[at].astype(f32) + (txf[at].astype(f32) + coarse_step * act)
        txu[at] = after.astype(bf16)
        upward[b].start()
        slope_o[at] = 1.0 - act * act

    @pl.when(first)
    def _():
        for b in range(bands):
            at = rows_of(b)
            txf[at] = ends[at].astype(bf16)
            put3(a3c, b * band, ends[at])
            across[b].start()
        if blocks > 2:
            for b in range(bands):
                pair_step(b)

    if blocks > 2:
        @pl.when(middle)
        def _():
            for b in range(bands + 2):
                if b < bands:
                    enter(b, upward)
                if 1 <= b <= bands:
                    own_step(b - 1, True)
                if b >= 2:
                    pair_step(b - 2)

        @pl.when(crown)
        def _():
            for b in range(bands + 1):
                if b < bands:
                    enter(b, upward)
                if b:
                    own_step(b - 1, True)
            for c in offset:
                c.wait_recv()
    else:
        @pl.when(first)
        def _():
            for c in offset:
                c.wait_recv()

    @pl.when(odd)
    def _():
        for b in range(bands + 1):
            if b < bands:
                enter(b, across)
            if b:
                own_step(b - 1, False)

    @pl.when(jnp.logical_not(first))
    def _():
        for i in range(1, depth):
            forward_layer(i)

    ends_copy = pltpu.make_async_copy(ends, ends_out, out_sem.at[0])
    ends_copy.start()
    pl.when(early)(turn_weights)

    for r in chunks:
        l = adj_ends[r : r + chunk]
        adj_starts[r : r + chunk] = l
        put3(a3s.at[top % 2], r, slope[top, r : r + chunk] * l)

    def adjoint_layer(i):
        now = i % 2
        for r in chunks:
            l = adj_starts[r : r + chunk] + step_size * conv(a3s.at[now], r, chunk, wt[i])
            adj_starts[r : r + chunk] = l
            if i:
                put3(a3s.at[1 - now], r, slope[i - 1, r : r + chunk] * l)

    for i in reversed(range(depth)):
        adjoint_layer(i)

    @pl.when(odd)
    def _():
        for b in range(bands):
            at = rows_of(b)
            txb[at] = adj_starts[at].astype(bf16)
            handed[b].start()

    pl.when(early)(turn_states)

    def leave(b):
        at = rows_of(b)
        downward[b].wait_recv()
        onward[b].start()
        put3(a3c, b * band, slope_o[at] * (ext[at].astype(f32) - adj_o[at]))

    def pair_back(b):
        at = rows_of(b)
        handed[b].wait_recv()
        diff = ext[at].astype(f32) - adj_o[at]
        exe[at] = rxb[at].astype(f32) + (diff + coarse_step * conv(a3c, b * band, band, wt_o[...]))

    def ready(b):
        at = rows_of(b)
        put3(a3s.at[0], b * band, slope[0, at] * (exe[at] - adj_ends[at]))

    def own_back(b):
        at = rows_of(b)
        out = adj_starts[at] + (
            exe[at] - adj_ends[at] + coarse_step * conv(a3s.at[0], b * band, band, wt[0])
        )
        txb[at] = out.astype(bf16)
        downward[b].start()

    def take_exit(b):
        at = rows_of(b)
        handed[b].wait_recv()
        exe[at] = rxb[at].astype(f32)

    if blocks > 2:
        @pl.when(crown)
        def _():
            for b in range(bands + 1):
                if b < bands:
                    take_exit(b)
                    ready(b)
                if b:
                    own_back(b - 1)

        @pl.when(middle)
        def _():
            for b in range(bands + 2):
                if b < bands:
                    leave(b)
                if 1 <= b <= bands:
                    pair_back(b - 1)
                    ready(b - 1)
                if b >= 2:
                    own_back(b - 2)

        @pl.when(first)
        def _():
            for b in range(bands + 1):
                if b < bands:
                    leave(b)
                if b:
                    pair_back(b - 1)
    else:
        @pl.when(first)
        def _():
            for b in range(bands):
                take_exit(b)

    @pl.when(even)
    def _():
        for r in chunks:
            adj_starts[r : r + chunk] = exe[r : r + chunk]

    @pl.when(jnp.logical_and(odd, jnp.logical_not(last)))
    def _():
        for c in onward:
            c.wait_recv()
        for r in chunks:
            adj_starts[r : r + chunk] = ext[r : r + chunk].astype(f32)

    @pl.when(last)
    def _():
        for r in chunks:
            adj_starts[r : r + chunk] = adj_ends[r : r + chunk]

    for r in chunks:
        put3(a3s.at[top % 2], r, slope[top, r : r + chunk] * adj_starts[r : r + chunk])
    pl.when(late)(turn_states)

    high, low = me // lows, lax.rem(me, lows)
    counts = ((lows, highs), (highs, lows))
    spots = ((low, high), (high, low))

    def turned(h, stage, d):
        c = list(spots[h])
        c[stage] = lax.rem(c[stage] + d + 1, counts[h][stage])
        return c

    def number(h, c):
        return c[1] * lows + c[0] if h == 0 else c[0] * lows + c[1]

    def wide(h, c):
        rows = half // counts[h][0]
        return pl.ds(pl.multiple_of(h * half + c[0] * rows, 16), rows)

    def narrow(h, c):
        rows = half // counts[h][0]
        return pl.ds(pl.multiple_of(h * half + c[0] * rows + c[1] * share, 16), share)

    def send(src, dst, ssem, rsem, to):
        return pltpu.make_async_remote_copy(
            src_ref=src, dst_ref=dst, send_sem=ssem, recv_sem=rsem,
            device_id={"dp": to}, device_id_type=MESH,
        )

    def one(g, h):
        rows = pl.ds(0, half // counts[h][0])
        for d in range(counts[h][0] - 1):
            c = turned(h, 0, d)
            yield send(gsend.at[g, wide(h, c)], rx1.at[g, h, d, rows],
                       one_send.at[g, h, d], one_recv.at[g, h, d], number(h, c))

    def two(g, h):
        for d in range(counts[h][1] - 1):
            c = turned(h, 1, d)
            src = pl.ds(pl.multiple_of(c[1] * share, 16), share)
            yield send(mid.at[g, h, src], rx2.at[g, h, d],
                       two_send.at[g, h, d], two_recv.at[g, h, d], number(h, c))

    def three(g, h):
        at = narrow(h, spots[h])
        for d in range(counts[h][1] - 1):
            yield send(gred.at[g, at], gred.at[g, at],
                       three_send.at[g, h, d], three_recv.at[g, h, d], number(h, turned(h, 1, d)))

    def four(g, h):
        at = wide(h, spots[h])
        for d in range(counts[h][0] - 1):
            yield send(gred.at[g, at], gred.at[g, at],
                       four_send.at[g, h, d], four_recv.at[g, h, d], number(h, turned(h, 0, d)))

    def start_one(g):
        for h in range(2):
            for c in one(g, h):
                c.start()

    def start_two(g):
        for h in range(2):
            for c in one(g, h):
                c.wait_recv()
            rows = half // counts[h][0]
            total = gsend[g, wide(h, spots[h])].astype(f32)
            for d in range(counts[h][0] - 1):
                total = total + rx1[g, h, d, 0:rows].astype(f32)
            mid[g, h, 0:rows] = total.astype(bf16)
            for c in two(g, h):
                c.start()

    def start_three(g):
        for h in range(2):
            for c in two(g, h):
                c.wait_recv()
            own = pl.ds(pl.multiple_of(spots[h][1] * share, 16), share)
            total = mid[g, h, own].astype(f32)
            for d in range(counts[h][1] - 1):
                total = total + rx2[g, h, d].astype(f32)
            gred[g, narrow(h, spots[h])] = total.astype(bf16)
            for c in three(g, h):
                c.start()

    def start_four(g):
        for h in range(2):
            for c in three(g, h):
                c.wait_recv()
            for c in four(g, h):
                c.start()

    def bias_copy(d):
        return pltpu.make_async_remote_copy(
            src_ref=bias_all.at[me], dst_ref=bias_all.at[me],
            send_sem=bi_send.at[d], recv_sem=bi_recv.at[d],
            device_id={"dp": peer[d]}, device_id_type=MESH,
        )

    for j in range(groups):
        g = groups - 1 - j
        for q in reversed(range(per_group)):
            i = g * per_group + q
            sig = a3s.at[i % 2]
            rhs = jnp.concatenate(
                [sig[(2 - e) * side : (2 - e) * side + pix, chans : 2 * chans] for e in range(3)], axis=1
            )
            found = jnp.dot(a3t[i], rhs, preferred_element_type=f32) * grad_scale
            for e in range(3):
                for d in range(3):
                    to = q * taps + (3 * e + d) * chans
                    gsend[g, to : to + chans] = found[
                        d * chans : (d + 1) * chans, e * chans : (e + 1) * chans
                    ].astype(bf16)
            summed = jnp.sum(sig[pad : pad + pix, chans : 2 * chans].astype(f32), axis=0, keepdims=True)
            brow[i] = summed * grad_scale
            if q == 0:
                start_one(g)
            adjoint_layer(i)

        for lag, stage in ((3, start_four), (2, start_three), (1, start_two)):
            if j >= lag:
                stage(g + lag)

    for i in range(depth):
        bias_all[me, i : i + 1] = brow[i]
    adj_copy = pltpu.make_async_copy(adj_starts, adj_out, out_sem.at[1])
    adj_copy.start()
    for d in range(peers - 1):
        bias_copy(d).start()
    for step in range(3):
        for lag, stage in ((3, start_four), (2, start_three), (1, start_two)):
            j = groups + step - lag
            if 0 <= j < groups:
                stage(groups - 1 - j)

    for d in range(peers - 1):
        bias_copy(d).wait_recv()
    total = bias_all[0, 0:depth]
    for p in range(1, peers):
        total = total + bias_all[p, 0:depth]
    bgrad[...] = total

    def grad_copy(g):
        return pltpu.make_async_copy(gred.at[g], wgrad_out.at[g], out_sem.at[2 + g])

    def finish(j, _):
        g = groups - 1 - j
        for h in range(2):
            for c in four(g, h):
                c.wait_recv()
        grad_copy(g).start()
        return 0

    lax.fori_loop(0, groups, finish, 0)

    def left(when, copies):
        @pl.when(when)
        def _():
            for c in copies:
                c.wait_send()

    left(even, across)
    left(odd, offset + handed + lent)
    left(rising, upward + onward)
    left(falling, downward)

    def drain(g, _):
        for h in range(2):
            for stage in (one, two, three, four):
                for c in stage(g, h):
                    c.wait_send()
        grad_copy(g).wait()
        return 0

    lax.fori_loop(0, groups, drain, 0)
    for d in range(peers - 1):
        bias_copy(d).wait_send()
    ends_copy.wait()
    adj_copy.wait()


def unpack(ends, adj_starts, wgrad, bgrad, ends_out, adj_out, wgrad_out, bgrad_out):
    ends_out[...] = ends[...]
    adj_out[...] = adj_starts[...]
    wgrad_out[...] = wgrad[...].astype(f32)
    bgrad_out[...] = bgrad[...]


def local(blocks, peers, starts, weights, biases, adj_ends):
    assert blocks % 2 == 0
    _, _, side, _, chans = starts.shape
    depth = weights.shape[0]
    pix = side * side
    taps = 9 * chans
    bands = 8
    chunk = min(256, pix)
    lows = min(n for n in range(1, peers + 1) if peers % n == 0 and n * n >= peers)
    highs = peers // lows
    groups = max(
        g for g in range(1, depth + 1)
        if depth % g == 0 and (depth // g * taps) % (32 * peers) == 0
    )
    group_rows = depth // groups * taps
    half = group_rows // 2
    slots = max(1, lows - 1, highs - 1)
    cfg = (blocks, peers, lows, depth, side, chans, groups, bands, chunk)
    padded = pix + 2 * side
    vmem = pl.BlockSpec(memory_space=pltpu.VMEM)
    anywhere = pl.BlockSpec(memory_space=pl.ANY)
    dma = pltpu.SemaphoreType.DMA
    others = peers - 1
    outs = pl.pallas_call(
        functools.partial(kernel, cfg),
        out_shape=(
            jax.ShapeDtypeStruct((pix, chans), f32),
            jax.ShapeDtypeStruct((pix, chans), f32),
            jax.ShapeDtypeStruct((groups, group_rows, chans), bf16),
            jax.ShapeDtypeStruct((depth, chans), f32),
        ),
        in_specs=[vmem] * 4,
        out_specs=(anywhere, anywhere, anywhere, vmem),
        scratch_shapes=[
            pltpu.VMEM((pix, chans), f32),
            pltpu.VMEM((pix, chans), f32),
            pltpu.VMEM((depth, padded, 3 * chans), bf16),
            pltpu.VMEM((2, padded, 3 * chans), bf16),
            pltpu.VMEM((depth, pix, chans), f32),
            pltpu.VMEM((pix, chans), f32),
            pltpu.VMEM((pix, chans), bf16),
            pltpu.VMEM((pix, chans), bf16),
            pltpu.VMEM((pix, chans), bf16),
            pltpu.VMEM((pix, chans), bf16),
            pltpu.VMEM((depth, taps, chans), bf16),
            pltpu.VMEM((depth, 3 * chans, pix), bf16),
            pltpu.VMEM((depth, 1, chans), f32),
            pltpu.VMEM((padded, 3 * chans), bf16),
            pltpu.VMEM((pix, chans), f32),
            pltpu.VMEM((pix, chans), bf16),
            pltpu.VMEM((pix, chans), bf16),
            pltpu.VMEM((pix, chans), f32),
            pltpu.VMEM((pix, chans), bf16),
            pltpu.VMEM((pix, chans), bf16),
            pltpu.VMEM((taps, chans), bf16),
            pltpu.VMEM((taps, chans), bf16),
            pltpu.VMEM((pix, chans), f32),
            pltpu.VMEM((8, chans), f32),
            pltpu.VMEM((8, chans), f32),
            pltpu.VMEM((groups, group_rows, chans), bf16),
            pltpu.VMEM((groups, 2, slots, half // min(lows, highs), chans), bf16),
            pltpu.VMEM((groups, 2, half // min(lows, highs), chans), bf16),
            pltpu.VMEM((groups, 2, slots, half // peers, chans), bf16),
            pltpu.VMEM((groups, group_rows, chans), bf16),
            pltpu.VMEM((peers, -(-depth // 8) * 8, chans), f32),
            *[dma((bands,))] * 12,
            dma((3,)), dma((3,)),
            *[dma((groups, 2, slots))] * 8,
            dma((max(1, others),)), dma((max(1, others),)),
            dma((2 + groups,)),
        ],
        compiler_params=pltpu.CompilerParams(
            collective_id=0, has_side_effects=True, vmem_limit_bytes=56 * 1024 * 1024
        ),
    )(
        starts.reshape(pix, chans), weights.reshape(depth, taps, chans), biases,
        adj_ends.reshape(pix, chans),
    )
    rows = pix // groups
    part = pl.BlockSpec((rows, chans), lambda g: (g, 0))
    block = pl.BlockSpec((1, group_rows, chans), lambda g: (g, 0, 0))
    whole = pl.BlockSpec((depth, chans), lambda g: (0, 0))
    specs = (part, part, block, whole)
    ends, adj_starts, wgrad, bgrad = pl.pallas_call(
        unpack,
        grid=(groups,),
        out_shape=tuple(jax.ShapeDtypeStruct(o.shape, f32) for o in outs),
        in_specs=list(specs),
        out_specs=specs,
        compiler_params=pltpu.CompilerParams(vmem_limit_bytes=60 * 1024 * 1024),
    )(*outs)
    return (
        ends.reshape(starts.shape), adj_starts.reshape(starts.shape),
        wgrad.reshape(weights.shape), bgrad,
    )


def solution(mesh):
    in_specs = (
        P("layer", "dp", None, None, None),
        P("layer", None, None, None),
        P("layer", None),
        P("layer", "dp", None, None, None),
    )
    out_specs = (
        P("layer", "dp", None, None, None),
        P("layer", "dp", None, None, None),
        P("layer", None, None, None),
        P("layer", None),
    )
    run = functools.partial(local, mesh.shape["layer"], mesh.shape["dp"])
    return jax.shard_map(run, mesh=mesh, in_specs=in_specs, out_specs=out_specs, check_vma=False)
```

```python
import functools
import math

import jax
import jax.numpy as jnp
from jax import lax
from jax.experimental import pallas as pl
from jax.experimental.pallas import tpu as pltpu
from jax.sharding import PartitionSpec as P

step_size = 0.25
MESH = pl.DeviceIdType.MESH
f32 = jnp.float32
bf16 = jnp.bfloat16


def kernel(
    cfg,
    starts, weights, biases, adj_ends,
    ends_out, adj_out, wgrad_out, bgrad,
    ends, adj_starts, a3f, a3s, slope, offs, ent, ext, txf, txb, wt, a3t, brow,
    a3c, slope_o, offs_o, rxb, exe, txu, txo, w_o, wt_o, adj_o, bias_o, bias_tx,
    gsend, rx1, mid, rx2, gred, bias_all,
    fsend, frecv, usend, urecv, osend, orecv, bsend, brecv, dsend, drecv, esend, erecv,
    msend, mrecv, one_send, one_recv, two_send, two_recv,
    three_send, three_recv, four_send, four_recv, bi_send, bi_recv, out_sem,
):
    blocks, peers, lows, depth, side, chans, groups, bands, chunk = cfg
    highs = peers // lows
    pix = side * side
    pad = side
    taps = 9 * chans
    per_group = depth // groups
    group_rows = per_group * taps
    half = group_rows // 2
    share = half // peers
    top = depth - 1
    coarse_step = depth * step_size
    grad_scale = 1.0 / (side * math.sqrt(peers))
    band = pix // bands

    k = lax.axis_index("layer")
    me = lax.axis_index("dp")
    first = k == 0
    last = k == blocks - 1
    peer = [lax.rem(me + d, peers) for d in range(1, peers)]

    barrier = pltpu.get_barrier_semaphore()

    even = lax.rem(k, 2) == 0
    odd = lax.rem(k, 2) == 1
    rising = jnp.logical_and(even, k < blocks - 2)
    falling = jnp.logical_and(even, k > 0)
    middle = jnp.logical_and(rising, k > 0)
    crown = k == blocks - 2

    def greet(when, to):
        @pl.when(when)
        def _():
            pl.semaphore_signal(barrier, inc=1, device_id={"layer": to}, device_id_type=MESH)

    greet(even, k + 1)
    greet(odd, k - 1)
    greet(rising, k + 2)
    greet(falling, k - 2)
    for p in peer:
        pl.semaphore_signal(barrier, inc=1, device_id={"dp": p}, device_id_type=MESH)
    greeted = peers + jnp.where(rising, 1, 0) + jnp.where(falling, 1, 0)

    def put3(dst, row, val):
        rows = val.shape[0]
        col = lax.rem(lax.broadcasted_iota(jnp.int32, (rows, chans), 0), side)
        before = jnp.where(col == 0, 0.0, pltpu.roll(val, 1, 0))
        after = jnp.where(col == side - 1, 0.0, pltpu.roll(val, rows - 1, 0))
        at = pl.ds(pad + row, rows)
        dst[at, 0:chans] = before.astype(bf16)
        dst[at, chans : 2 * chans] = val.astype(bf16)
        dst[at, 2 * chans : 3 * chans] = after.astype(bf16)

    def conv(src, row, rows, mat):
        lhs = jnp.concatenate([src[pl.ds(row + e * side, rows), :] for e in range(3)], axis=1)
        return jnp.dot(lhs, mat, preferred_element_type=f32)

    bias32 = biases[...].astype(f32)
    for i in range(depth):
        brow[i] = bias32[i : i + 1]
    zeros = jnp.zeros((pad, 3 * chans), bf16)
    for i in range(depth):
        a3f[i, 0:pad] = zeros
        a3f[i, pad + pix : 2 * pad + pix] = zeros
    for i in range(2):
        a3s[i, 0:pad] = zeros
        a3s[i, pad + pix : 2 * pad + pix] = zeros

    a3c[0:pad] = zeros
    a3c[pad + pix : 2 * pad + pix] = zeros
    bias_tx[...] = jnp.broadcast_to(bias32[0:1], bias_tx.shape)

    chunks = list(range(0, pix, chunk))

    def hop(src, dst, send, recv, b, to):
        at = pl.ds(b * band, band)
        return pltpu.make_async_remote_copy(
            src_ref=src.at[at], dst_ref=dst.at[at], send_sem=send.at[b], recv_sem=recv.at[b],
            device_id={"layer": to}, device_id_type=MESH,
        )

    def to_partner(src, dst, n):
        return pltpu.make_async_remote_copy(
            src_ref=src, dst_ref=dst, send_sem=msend.at[n], recv_sem=mrecv.at[n],
            device_id={"layer": jnp.maximum(k - 1, 0)}, device_id_type=MESH,
        )

    def along(src, dst, send, recv, by):
        to = lax.rem(k + by + blocks, blocks)
        return [hop(src, dst, send, recv, b, to) for b in range(bands)]

    across = along(txf, ent, fsend, frecv, 1)
    upward = along(txu, ent, usend, urecv, 2)
    offset = along(txo, offs_o, osend, orecv, -1)
    handed = along(txb, rxb, bsend, brecv, -1)
    downward = along(txb, ext, dsend, drecv, -2)
    onward = along(ext, ext, esend, erecv, 1)
    lent = [to_partner(weights.at[0], w_o, 0), to_partner(bias_tx, bias_o, 1), to_partner(adj_ends, adj_o, 2)]

    for r in chunks:
        put3(a3f.at[0], r, starts[r : r + chunk])
    for r in chunks:
        act = jnp.tanh(conv(a3f.at[0], r, chunk, weights[0]) + brow[0])
        slope[0, r : r + chunk] = 1.0 - act * act
        u0 = starts[r : r + chunk]
        u1 = u0 + step_size * act
        offs[r : r + chunk] = u0 + coarse_step * act
        ends[r : r + chunk] = u1
        if top:
            put3(a3f.at[1], r, u1)

    pl.semaphore_wait(barrier, greeted)

    @pl.when(odd)
    def _():
        for c in lent:
            c.start()

    def forward_layer(i):
        for r in chunks:
            act = jnp.tanh(conv(a3f.at[i], r, chunk, weights[i]) + brow[i])
            slope[i, r : r + chunk] = 1.0 - act * act
            u = ends[r : r + chunk] + step_size * act
            ends[r : r + chunk] = u
            if i < top:
                put3(a3f.at[i + 1], r, u)

    for i in range(1, depth):
        forward_layer(i)
    for r in chunks:
        offs[r : r + chunk] = ends[r : r + chunk] - offs[r : r + chunk]
        txo[r : r + chunk] = offs[r : r + chunk].astype(bf16)

    @pl.when(odd)
    def _():
        for c in offset:
            c.start()

    @pl.when(even)
    def _():
        for c in lent:
            c.wait_recv()

    def turn_weights():
        def one(i, _):
            for t in range(9):
                wt[i, t * chans : (t + 1) * chans] = weights[i, (8 - t) * chans : (9 - t) * chans].T
            return 0

        lax.fori_loop(0, depth, one, 0)

        @pl.when(even)
        def _():
            for t in range(9):
                wt_o[t * chans : (t + 1) * chans] = w_o[(8 - t) * chans : (9 - t) * chans].T

    def turn_states():
        def one(i, _):
            for d in range(3):
                for r in range(0, pix, chans):
                    a3t[i, d * chans : (d + 1) * chans, r : r + chans] = a3f[
                        i, pad + r : pad + r + chans, d * chans : (d + 1) * chans
                    ].T
            return 0

        lax.fori_loop(0, depth, one, 0)

    early = k < blocks // 2
    late = jnp.logical_not(early)
    pl.when(late)(turn_weights)

    def rows_of(b):
        return pl.ds(b * band, band)

    def enter(b, copies):
        copies[b].wait_recv()
        put3(a3f.at[0], b * band, ent[rows_of(b)].astype(f32))

    def own_step(b, passes):
        at = rows_of(b)
        act = jnp.tanh(conv(a3f.at[0], b * band, band, weights[0]) + brow[0])
        state = ent[at].astype(f32)
        if passes:
            after = offs[at] + (state + coarse_step * act)
            txf[at] = after.astype(bf16)
            put3(a3c, b * band, after)
            across[b].start()
        slope[0, at] = 1.0 - act * act
        u = state + step_size * act
        ends[at] = u
        if top:
            put3(a3f.at[1], b * band, u)

    def pair_step(b):
        at = rows_of(b)
        offset[b].wait_recv()
        act = jnp.tanh(conv(a3c, b * band, band, w_o[...]) + bias_o[0:1])
        after = offs_o[at].astype(f32) + (txf[at].astype(f32) + coarse_step * act)
        txu[at] = after.astype(bf16)
        upward[b].start()
        slope_o[at] = 1.0 - act * act

    @pl.when(first)
    def _():
        for b in range(bands):
            at = rows_of(b)
            txf[at] = ends[at].astype(bf16)
            put3(a3c, b * band, ends[at])
            across[b].start()
        if blocks > 2:
            for b in range(bands):
                pair_step(b)

    if blocks > 2:
        @pl.when(middle)
        def _():
            for b in range(bands + 2):
                if b < bands:
                    enter(b, upward)
                if 1 <= b <= bands:
                    own_step(b - 1, True)
                if b >= 2:
                    pair_step(b - 2)

        @pl.when(crown)
        def _():
            for b in range(bands + 1):
                if b < bands:
                    enter(b, upward)
                if b:
                    own_step(b - 1, True)
            for c in offset:
                c.wait_recv()
    else:
        @pl.when(first)
        def _():
            for c in offset:
                c.wait_recv()

    @pl.when(odd)
    def _():
        for b in range(bands + 1):
            if b < bands:
                enter(b, across)
            if b:
                own_step(b - 1, False)

    @pl.when(jnp.logical_not(first))
    def _():
        for i in range(1, depth):
            forward_layer(i)

    ends_copy = pltpu.make_async_copy(ends, ends_out, out_sem.at[0])
    ends_copy.start()
    pl.when(early)(turn_weights)

    for r in chunks:
        l = adj_ends[r : r + chunk]
        adj_starts[r : r + chunk] = l
        put3(a3s.at[top % 2], r, slope[top, r : r + chunk] * l)

    def adjoint_layer(i):
        now = i % 2
        for r in chunks:
            l = adj_starts[r : r + chunk] + step_size * conv(a3s.at[now], r, chunk, wt[i])
            adj_starts[r : r + chunk] = l
            if i:
                put3(a3s.at[1 - now], r, slope[i - 1, r : r + chunk] * l)

    for i in reversed(range(depth)):
        adjoint_layer(i)

    @pl.when(odd)
    def _():
        for b in range(bands):
            at = rows_of(b)
            txb[at] = adj_starts[at].astype(bf16)
            handed[b].start()

    pl.when(early)(turn_states)

    def leave(b):
        at = rows_of(b)
        downward[b].wait_recv()
        onward[b].start()
        put3(a3c, b * band, slope_o[at] * (ext[at].astype(f32) - adj_o[at]))

    def pair_back(b):
        at = rows_of(b)
        handed[b].wait_recv()
        diff = ext[at].astype(f32) - adj_o[at]
        exe[at] = rxb[at].astype(f32) + (diff + coarse_step * conv(a3c, b * band, band, wt_o[...]))

    def ready(b):
        at = rows_of(b)
        put3(a3s.at[0], b * band, slope[0, at] * (exe[at] - adj_ends[at]))

    def own_back(b):
        at = rows_of(b)
        out = adj_starts[at] + (
            exe[at] - adj_ends[at] + coarse_step * conv(a3s.at[0], b * band, band, wt[0])
        )
        txb[at] = out.astype(bf16)
        downward[b].start()

    def take_exit(b):
        at = rows_of(b)
        handed[b].wait_recv()
        exe[at] = rxb[at].astype(f32)

    if blocks > 2:
        @pl.when(crown)
        def _():
            for b in range(bands + 1):
                if b < bands:
                    take_exit(b)
                    ready(b)
                if b:
                    own_back(b - 1)

        @pl.when(middle)
        def _():
            for b in range(bands + 2):
                if b < bands:
                    leave(b)
                if 1 <= b <= bands:
                    pair_back(b - 1)
                    ready(b - 1)
                if b >= 2:
                    own_back(b - 2)

        @pl.when(first)
        def _():
            for b in range(bands + 1):
                if b < bands:
                    leave(b)
                if b:
                    pair_back(b - 1)
    else:
        @pl.when(first)
        def _():
            for b in range(bands):
                take_exit(b)

    @pl.when(even)
    def _():
        for r in chunks:
            adj_starts[r : r + chunk] = exe[r : r + chunk]

    @pl.when(jnp.logical_and(odd, jnp.logical_not(last)))
    def _():
        for c in onward:
            c.wait_recv()
        for r in chunks:
            adj_starts[r : r + chunk] = ext[r : r + chunk].astype(f32)

    @pl.when(last)
    def _():
        for r in chunks:
            adj_starts[r : r + chunk] = adj_ends[r : r + chunk]

    for r in chunks:
        put3(a3s.at[top % 2], r, slope[top, r : r + chunk] * adj_starts[r : r + chunk])
    pl.when(late)(turn_states)

    high, low = me // lows, lax.rem(me, lows)
    counts = ((lows, highs), (highs, lows))
    spots = ((low, high), (high, low))

    def turned(h, stage, d):
        c = list(spots[h])
        c[stage] = lax.rem(c[stage] + d + 1, counts[h][stage])
        return c

    def number(h, c):
        return c[1] * lows + c[0] if h == 0 else c[0] * lows + c[1]

    def wide(h, c):
        rows = half // counts[h][0]
        return pl.ds(pl.multiple_of(h * half + c[0] * rows, 16), rows)

    def narrow(h, c):
        rows = half // counts[h][0]
        return pl.ds(pl.multiple_of(h * half + c[0] * rows + c[1] * share, 16), share)

    def send(src, dst, ssem, rsem, to):
        return pltpu.make_async_remote_copy(
            src_ref=src, dst_ref=dst, send_sem=ssem, recv_sem=rsem,
            device_id={"dp": to}, device_id_type=MESH,
        )

    def one(g, h):
        rows = pl.ds(0, half // counts[h][0])
        for d in range(counts[h][0] - 1):
            c = turned(h, 0, d)
            yield send(gsend.at[g, wide(h, c)], rx1.at[g, h, d, rows],
                       one_send.at[g, h, d], one_recv.at[g, h, d], number(h, c))

    def two(g, h):
        for d in range(counts[h][1] - 1):
            c = turned(h, 1, d)
            src = pl.ds(pl.multiple_of(c[1] * share, 16), share)
            yield send(mid.at[g, h, src], rx2.at[g, h, d],
                       two_send.at[g, h, d], two_recv.at[g, h, d], number(h, c))

    def three(g, h):
        at = narrow(h, spots[h])
        for d in range(counts[h][1] - 1):
            yield send(gred.at[g, at], gred.at[g, at],
                       three_send.at[g, h, d], three_recv.at[g, h, d], number(h, turned(h, 1, d)))

    def four(g, h):
        at = wide(h, spots[h])
        for d in range(counts[h][0] - 1):
            yield send(gred.at[g, at], gred.at[g, at],
                       four_send.at[g, h, d], four_recv.at[g, h, d], number(h, turned(h, 0, d)))

    def start_one(g):
        for h in range(2):
            for c in one(g, h):
                c.start()

    def start_two(g):
        for h in range(2):
            for c in one(g, h):
                c.wait_recv()
            rows = half // counts[h][0]
            total = gsend[g, wide(h, spots[h])].astype(f32)
            for d in range(counts[h][0] - 1):
                total = total + rx1[g, h, d, 0:rows].astype(f32)
            mid[g, h, 0:rows] = total.astype(bf16)
            for c in two(g, h):
                c.start()

    def start_three(g):
        for h in range(2):
            for c in two(g, h):
                c.wait_recv()
            own = pl.ds(pl.multiple_of(spots[h][1] * share, 16), share)
            total = mid[g, h, own].astype(f32)
            for d in range(counts[h][1] - 1):
                total = total + rx2[g, h, d].astype(f32)
            gred[g, narrow(h, spots[h])] = total.astype(bf16)
            for c in three(g, h):
                c.start()

    def start_four(g):
        for h in range(2):
            for c in three(g, h):
                c.wait_recv()
            for c in four(g, h):
                c.start()

    def bias_copy(d):
        return pltpu.make_async_remote_copy(
            src_ref=bias_all.at[me], dst_ref=bias_all.at[me],
            send_sem=bi_send.at[d], recv_sem=bi_recv.at[d],
            device_id={"dp": peer[d]}, device_id_type=MESH,
        )

    for j in range(groups):
        g = groups - 1 - j
        for q in reversed(range(per_group)):
            i = g * per_group + q
            sig = a3s.at[i % 2]
            rhs = jnp.concatenate(
                [sig[(2 - e) * side : (2 - e) * side + pix, chans : 2 * chans] for e in range(3)], axis=1
            )
            found = jnp.dot(a3t[i], rhs, preferred_element_type=f32) * grad_scale
            for e in range(3):
                for d in range(3):
                    to = q * taps + (3 * e + d) * chans
                    gsend[g, to : to + chans] = found[
                        d * chans : (d + 1) * chans, e * chans : (e + 1) * chans
                    ].astype(bf16)
            summed = jnp.sum(sig[pad : pad + pix, chans : 2 * chans].astype(f32), axis=0, keepdims=True)
            brow[i] = summed * grad_scale
            if q == 0:
                start_one(g)
            adjoint_layer(i)

        for lag, stage in ((3, start_four), (2, start_three), (1, start_two)):
            if j >= lag:
                stage(g + lag)

    for i in range(depth):
        bias_all[me, i : i + 1] = brow[i]
    adj_copy = pltpu.make_async_copy(adj_starts, adj_out, out_sem.at[1])
    adj_copy.start()
    for d in range(peers - 1):
        bias_copy(d).start()
    for step in range(3):
        for lag, stage in ((3, start_four), (2, start_three), (1, start_two)):
            j = groups + step - lag
            if 0 <= j < groups:
                stage(groups - 1 - j)

    for d in range(peers - 1):
        bias_copy(d).wait_recv()
    total = bias_all[0, 0:depth]
    for p in range(1, peers):
        total = total + bias_all[p, 0:depth]
    bgrad[...] = total

    def grad_copy(g):
        return pltpu.make_async_copy(gred.at[g], wgrad_out.at[g], out_sem.at[2 + g])

    def finish(j, _):
        g = groups - 1 - j
        for h in range(2):
            for c in four(g, h):
                c.wait_recv()
        grad_copy(g).start()
        return 0

    lax.fori_loop(0, groups, finish, 0)

    def left(when, copies):
        @pl.when(when)
        def _():
            for c in copies:
                c.wait_send()

    left(even, across)
    left(odd, offset + handed + lent)
    left(rising, upward + onward)
    left(falling, downward)

    def drain(g, _):
        for h in range(2):
            for stage in (one, two, three, four):
                for c in stage(g, h):
                    c.wait_send()
        grad_copy(g).wait()
        return 0

    lax.fori_loop(0, groups, drain, 0)
    for d in range(peers - 1):
        bias_copy(d).wait_send()
    ends_copy.wait()
    adj_copy.wait()


def unpack(ends, adj_starts, wgrad, bgrad, ends_out, adj_out, wgrad_out, bgrad_out, sems):
    copies = [
        pltpu.make_async_copy(ends, ends_out, sems.at[0]),
        pltpu.make_async_copy(adj_starts, adj_out, sems.at[1]),
    ]

    @pl.when(pl.program_id(0) == 0)
    def _():
        for c in copies:
            c.start()

    wgrad_out[...] = wgrad[...].astype(f32)
    bgrad_out[...] = bgrad[...]

    @pl.when(pl.program_id(0) == pl.num_programs(0) - 1)
    def _():
        for c in copies:
            c.wait()


def local(blocks, peers, starts, weights, biases, adj_ends):
    assert blocks % 2 == 0
    _, _, side, _, chans = starts.shape
    depth = weights.shape[0]
    pix = side * side
    taps = 9 * chans
    bands = 4
    chunk = min(256, pix)
    lows = min(n for n in range(1, peers + 1) if peers % n == 0 and n * n >= peers)
    highs = peers // lows
    groups = max(
        g for g in range(1, depth + 1)
        if depth % g == 0 and (depth // g * taps) % (32 * peers) == 0
    )
    group_rows = depth // groups * taps
    half = group_rows // 2
    slots = max(1, lows - 1, highs - 1)
    cfg = (blocks, peers, lows, depth, side, chans, groups, bands, chunk)
    padded = pix + 2 * side
    vmem = pl.BlockSpec(memory_space=pltpu.VMEM)
    anywhere = pl.BlockSpec(memory_space=pl.ANY)
    dma = pltpu.SemaphoreType.DMA
    others = peers - 1
    outs = pl.pallas_call(
        functools.partial(kernel, cfg),
        out_shape=(
            jax.ShapeDtypeStruct((pix, chans), f32),
            jax.ShapeDtypeStruct((pix, chans), f32),
            jax.ShapeDtypeStruct((groups, group_rows, chans), bf16),
            jax.ShapeDtypeStruct((depth, chans), f32),
        ),
        in_specs=[vmem] * 4,
        out_specs=(anywhere, anywhere, anywhere, vmem),
        scratch_shapes=[
            pltpu.VMEM((pix, chans), f32),
            pltpu.VMEM((pix, chans), f32),
            pltpu.VMEM((depth, padded, 3 * chans), bf16),
            pltpu.VMEM((2, padded, 3 * chans), bf16),
            pltpu.VMEM((depth, pix, chans), f32),
            pltpu.VMEM((pix, chans), f32),
            pltpu.VMEM((pix, chans), bf16),
            pltpu.VMEM((pix, chans), bf16),
            pltpu.VMEM((pix, chans), bf16),
            pltpu.VMEM((pix, chans), bf16),
            pltpu.VMEM((depth, taps, chans), bf16),
            pltpu.VMEM((depth, 3 * chans, pix), bf16),
            pltpu.VMEM((depth, 1, chans), f32),
            pltpu.VMEM((padded, 3 * chans), bf16),
            pltpu.VMEM((pix, chans), f32),
            pltpu.VMEM((pix, chans), bf16),
            pltpu.VMEM((pix, chans), bf16),
            pltpu.VMEM((pix, chans), f32),
            pltpu.VMEM((pix, chans), bf16),
            pltpu.VMEM((pix, chans), bf16),
            pltpu.VMEM((taps, chans), bf16),
            pltpu.VMEM((taps, chans), bf16),
            pltpu.VMEM((pix, chans), f32),
            pltpu.VMEM((8, chans), f32),
            pltpu.VMEM((8, chans), f32),
            pltpu.VMEM((groups, group_rows, chans), bf16),
            pltpu.VMEM((groups, 2, slots, half // min(lows, highs), chans), bf16),
            pltpu.VMEM((groups, 2, half // min(lows, highs), chans), bf16),
            pltpu.VMEM((groups, 2, slots, half // peers, chans), bf16),
            pltpu.VMEM((groups, group_rows, chans), bf16),
            pltpu.VMEM((peers, -(-depth // 8) * 8, chans), f32),
            *[dma((bands,))] * 12,
            dma((3,)), dma((3,)),
            *[dma((groups, 2, slots))] * 8,
            dma((max(1, others),)), dma((max(1, others),)),
            dma((2 + groups,)),
        ],
        compiler_params=pltpu.CompilerParams(
            collective_id=0, has_side_effects=True, vmem_limit_bytes=56 * 1024 * 1024
        ),
    )(
        starts.reshape(pix, chans), weights.reshape(depth, taps, chans), biases,
        adj_ends.reshape(pix, chans),
    )
    block = pl.BlockSpec((1, group_rows, chans), lambda g: (g, 0, 0))
    whole = pl.BlockSpec((depth, chans), lambda g: (0, 0))
    specs = (anywhere, anywhere, block, whole)
    ends, adj_starts, wgrad, bgrad = pl.pallas_call(
        unpack,
        grid=(groups,),
        out_shape=tuple(jax.ShapeDtypeStruct(o.shape, f32) for o in outs),
        in_specs=list(specs),
        out_specs=specs,
        scratch_shapes=[dma((2,))],
        compiler_params=pltpu.CompilerParams(vmem_limit_bytes=60 * 1024 * 1024),
    )(*outs)
    return (
        ends.reshape(starts.shape), adj_starts.reshape(starts.shape),
        wgrad.reshape(weights.shape), bgrad,
    )


def solution(mesh):
    in_specs = (
        P("layer", "dp", None, None, None),
        P("layer", None, None, None),
        P("layer", None),
        P("layer", "dp", None, None, None),
    )
    out_specs = (
        P("layer", "dp", None, None, None),
        P("layer", "dp", None, None, None),
        P("layer", None, None, None),
        P("layer", None),
    )
    run = functools.partial(local, mesh.shape["layer"], mesh.shape["dp"])
    return jax.shard_map(run, mesh=mesh, in_specs=in_specs, out_specs=out_specs, check_vma=False)
```
